256 devices in a mesh: section: 8 (over x_lo, y), seq: 16 (over z, core), dp: 2 (over x_hi).
Axes of the slice: x: 4 (x_hi: 2, x_lo: 2; x = x_hi * 2 + x_lo), y: 4, z: 8, core: 2. Of those that a mesh axis runs over, the one named last changes fastest.
Arguments:
- mel: bfloat16 [4, 8192, 128], P('dp', 'seq'), may hold values from -6 to 6
- lengths: int32 [4], P('dp'), may hold values from 1024 to 2048, as said below
- stem_weight: bfloat16 [512, 1536], P(('seq', 'dp')), may hold values from -0.25 to 0.25
- w_qkv: bfloat16 [8, 1536, 2304], P('section', ('seq', 'dp'))
- w_out: bfloat16 [8, 768, 1536], P('section', ('seq', 'dp')), may hold values from -0.21875 to 0.21875
- norm_gains: float32 [8, 2, 1536], P('section'), may hold values from 0.25 to 1.75
- conv_kernel: float32 [8, 5, 1536], P('section'), may hold values from -2.5 to 2.5
Outputs:
- arrivals: bfloat16 [8, 4, 2048, 1536], P('section', 'dp', 'seq')
The draws below stay inside these ranges and needn't reach their ends.
Inputs may be any that keep to these rules, and one draw needn't show every extreme that they name: `lengths`: every utterance keeps at least half of its 2048 frames; one utterance of each draw keeps all of them.
All inputs are finite; a program needn't handle non-finite values.
Results may differ from the reference program's by a relative error of at most 0.029.
Values may be sent and summed in bfloat16 or wider, within the bound.
A program may use at most 64 MiB of HBM per device.

```python
import jax
import jax.numpy as jnp
from jax import lax

D = 1536
HEADS = 8
HD = 96
MEL = 128
STRIDE = 4
KW = 5
FRAMES_DEV = 128
FRAMES = 2048
UTTS = 4
HH = 768
N_SECTION = 8


def draw_lengths(key, part):
    key = jax.random.fold_in(key, 11)
    draw_key, pick_key = jax.random.split(key)
    drawn = jax.random.randint(draw_key, (UTTS,), FRAMES // 2, FRAMES + 1, dtype=jnp.int32)
    full_index = jax.random.randint(pick_key, (), 0, UTTS, dtype=jnp.int32)
    return jnp.where(jnp.arange(UTTS, dtype=jnp.int32) == full_index, FRAMES, drawn).astype(jnp.int32)


def draw_w_qkv(key, part):
    key = jax.random.fold_in(key, 23)
    width = HEADS * HD
    base = jax.random.normal(key, (N_SECTION, D, 3 * width), jnp.float32) * D ** (-0.5)
    return base.astype(jnp.bfloat16)


def levels(own_key, dims, shards, least, largest):
    loudness, own = 1.0, jax.random.fold_in(own_key, 6)
    for position, blocks in shards:
        steps = jnp.exp(jax.random.uniform(jax.random.fold_in(own, position), (blocks,), jnp.float32, least / len(shards), largest / len(shards)))
        loudness = loudness * jnp.repeat(steps, dims[position] // blocks).reshape([-1 if axis == position else 1 for axis in range(len(dims))])
    return loudness


def scatter_about(key, shape, scale, most, pieces=(), kind=jnp.bfloat16):
    values = jax.random.normal(key, shape, jnp.float32) * scale
    if len(pieces) > 0:
        values = levels(key, shape, pieces, -0.22, 0.18) * values
    return jnp.clip(values, min=-most, max=most).astype(kind)


def setup_inputs(seed: int = 0) -> dict:
    keys = jax.random.split(jax.random.key(seed), 8)
    mel = scatter_about(keys[0], (UTTS, STRIDE * FRAMES, MEL), 1.0, 6.0, ((0, 2), (1, 16)))
    lengths = draw_lengths(jax.random.fold_in(keys[7], 71), 0)
    stem_weight = scatter_about(keys[2], (STRIDE * MEL, D), (STRIDE * MEL) ** -0.5, 0.25, ((0, 32),))
    w_qkv = draw_w_qkv(jax.random.fold_in(keys[7], 71), 0)
    w_out = scatter_about(keys[4], (N_SECTION, HH, D), HH ** -0.5, 0.21875, ((0, 8), (1, 32)))
    norm_gains = jnp.clip(1.0 + 0.15 * jax.random.normal(keys[5], (N_SECTION, 2, D), jnp.float32), 0.25, 1.75)
    conv_kernel = scatter_about(keys[6], (N_SECTION, KW, D), KW ** -0.5, 2.5, ((0, 8),), jnp.float32)
    return {"mel": mel, "lengths": lengths, "stem_weight": stem_weight, "w_qkv": w_qkv, "w_out": w_out, "norm_gains": norm_gains, "conv_kernel": conv_kernel}


eps = 1e-05
masked_score = -1e+30

def layer_norm(value, gain):
    average = lax.optimization_barrier(jnp.mean(value, axis=-1, keepdims=True))
    centered = value - average
    variance = lax.optimization_barrier(jnp.mean(centered * centered, axis=-1, keepdims=True))
    return centered * lax.rsqrt(variance + eps) * gain

def band_attention(queries, keys_values, first_query, length, heads):
    frames = queries.shape[0]
    width = queries.shape[1]
    head_size = width // heads
    span = keys_values.shape[0]
    query_rows = queries.reshape(frames, heads, head_size).astype(jnp.float32)
    key_rows = keys_values[:, :width].reshape(span, heads, head_size).astype(jnp.float32)
    value_rows = keys_values[:, width:].reshape(span, heads, head_size).astype(jnp.float32)
    scores = jnp.einsum('qhd,khd->hqk', query_rows, key_rows) * (1.0 / head_size ** 0.5)
    query_pos = first_query + jnp.arange(frames, dtype=jnp.int32)
    key_pos = first_query - frames + jnp.arange(span, dtype=jnp.int32)
    allowed = (key_pos[None, :] >= 0) & (key_pos[None, :] < length) & (jnp.abs(query_pos[:, None] - key_pos[None, :]) <= frames)
    scores = jnp.where(allowed[None], scores, masked_score)
    highest = lax.optimization_barrier(jnp.max(scores, axis=-1, keepdims=True))
    expon = jnp.exp(scores - highest)
    probs = (expon / lax.optimization_barrier(jnp.sum(expon, axis=-1, keepdims=True))).astype(jnp.bfloat16)
    context = jnp.einsum('hqk,khd->qhd', probs.astype(jnp.float32), value_rows)
    return context.astype(jnp.bfloat16).reshape(frames, width)

def attention_all(qkv, length):
    width = HEADS * HD
    padded = jnp.pad(qkv[:, width:], ((FRAMES_DEV, FRAMES_DEV), (0, 0)))

    def one_block(block):
        first_query = (block * FRAMES_DEV).astype(jnp.int32)
        queries = lax.dynamic_slice_in_dim(qkv[:, :width], first_query, FRAMES_DEV, 0)
        nearby = lax.dynamic_slice_in_dim(padded, first_query, 3 * FRAMES_DEV, 0)
        return band_attention(queries, nearby, first_query, length, HEADS)
    blocks = lax.map(one_block, jnp.arange(FRAMES // FRAMES_DEV, dtype=jnp.int32))
    return blocks.reshape(FRAMES, width)

def apply_layer(held_input, valid, length, layer_qkv, layer_out, gains, kernel):
    stream = held_input.astype(jnp.float32)
    normed = layer_norm(stream, gains[0]).astype(jnp.bfloat16)
    qkv = jnp.dot(normed, layer_qkv, preferred_element_type=jnp.float32).astype(jnp.bfloat16)
    context = attention_all(qkv, length)
    stream = stream + jnp.dot(context, layer_out, preferred_element_type=jnp.float32)
    conv_in = (layer_norm(stream, gains[1]) * valid[:, None]).astype(jnp.bfloat16)
    rim_width = KW // 2
    padded = jnp.pad(conv_in, ((rim_width, rim_width), (0, 0)))
    conv = jnp.zeros(stream.shape, jnp.float32)
    for offset in range(KW):
        conv = conv + padded[offset:offset + FRAMES].astype(jnp.float32) * kernel[offset]
    return ((stream + jax.nn.silu(conv)) * valid[:, None]).astype(jnp.bfloat16)

def reference(mel, lengths, stem_weight, w_qkv, w_out, norm_gains, conv_kernel):
    results = []
    for utterance in range(UTTS):
        length = lengths[utterance]
        valid = (jnp.arange(FRAMES, dtype=jnp.int32) < length).astype(jnp.float32)
        grouped = mel[utterance].reshape(FRAMES, STRIDE * MEL)
        stem_out = jax.nn.silu(jnp.dot(grouped, stem_weight, preferred_element_type=jnp.float32))
        held_input = (stem_out * valid[:, None]).astype(jnp.bfloat16)
        collected = [None] * N_SECTION
        for layer in range(N_SECTION):
            held_input = apply_layer(held_input, valid, length, w_qkv[layer], w_out[layer], norm_gains[layer], conv_kernel[layer])
            collected[(layer + 1) % N_SECTION] = held_input
        results.append(jnp.stack(collected))
    return jnp.stack(results, axis=1)
```

```python
import functools

import jax
import jax.numpy as jnp
from jax import lax
from jax.experimental import pallas as pl
from jax.experimental.pallas import tpu as pltpu
from jax.sharding import PartitionSpec as P

HEADS = 8
STRIDE = 4
CHUNKS = 4
eps = 1e-05
masked_score = -1e30
F32 = jnp.float32
BF16 = jnp.bfloat16
MESH = pl.DeviceIdType.MESH


def remote(src, dst, send, recv, **device):
    return pltpu.make_async_remote_copy(
        src_ref=src, dst_ref=dst, send_sem=send, recv_sem=recv, device_id=device, device_id_type=MESH
    )


def rows(ref, start, count):
    return ref.at[pl.ds(pl.multiple_of(start, 16), count)]


def kernel(
    sections, nseq,
    lengths, grouped, stem_in, qkv_in, out_in, gains, taps, arrivals,
    stem_full, qkv_full, out_full, out_peer, xs, normed, kv, queries, context, mask, stream, conv_in, result,
    local_sem, pair_send, pair_recv, ring_send, ring_recv, cross_send, cross_recv,
    halo_send, halo_recv, rim_send, rim_recv, relay_send, relay_recv, done_sem,
):
    section = lax.axis_index("section")
    seq = lax.axis_index("seq")
    dp = lax.axis_index("dp")
    nz = nseq // 2
    z, core = seq // 2, seq % 2
    ahead = ((z + 1) % nz) * 2 + core
    behind = ((z + nz - 1) % nz) * 2 + core
    other = seq + 1 - 2 * core
    right, left = (seq + 1) % nseq, (seq + nseq - 1) % nseq
    far = jnp.where(core == 1, right, left)
    following, preceding = (section + 1) % sections, (section + sections - 1) % sections
    first = section == 0

    micro, frames, width = xs.shape[0] // 2, xs.shape[1], xs.shape[2]
    heads_width = queries.shape[1]
    head_size = heads_width // HEADS
    stem_rows, qkv_rows, out_rows = stem_in.shape[0], qkv_in.shape[0], out_in.shape[0]

    barrier = pltpu.get_barrier_semaphore()
    for device in (
        {"seq": ahead}, {"seq": behind}, {"seq": other}, {"seq": far},
        {"dp": 1 - dp}, {"section": following}, {"section": preceding},
    ):
        pl.semaphore_signal(barrier, inc=1, device_id=device, device_id_type=MESH)
    pl.semaphore_wait(barrier, 7)

    def own_rows(full, count):
        return rows(full, (seq * 2 + dp) * count, count)

    stem_pair = remote(stem_in, own_rows(stem_full, stem_rows), pair_send.at[2], pair_recv.at[2], dp=1 - dp)
    stem_keep = pltpu.make_async_copy(stem_in, own_rows(stem_full, stem_rows), local_sem.at[1])
    qkv_pair = remote(qkv_in, own_rows(qkv_full, qkv_rows), pair_send.at[0], pair_recv.at[0], dp=1 - dp)
    qkv_keep = pltpu.make_async_copy(qkv_in, own_rows(qkv_full, qkv_rows), local_sem.at[0])
    out_pair = remote(out_in, out_peer, pair_send.at[1], pair_recv.at[1], dp=1 - dp)

    @pl.when(first)
    def _():
        stem_pair.start()
        stem_keep.start()

    qkv_pair.start()
    qkv_keep.start()
    out_pair.start()

    def block(full, count, zz, cc, low=0, high=None):
        high = count if high is None else high
        return rows(full, (zz * 2 + cc) * count + low, high - low)

    steps = nz // 2

    def ring(arrays, beside=None):
        sent = []
        for t in range(steps):
            last = t == steps - 1
            zf, zb = (z + nz - t) % nz, (z + t) % nz
            moves = []
            for index, full, count, cut in arrays:
                src = block(full, count, zf, core, 0, cut if last else count)
                moves.append(remote(src, src, ring_send.at[index, 0, t], ring_recv.at[index, 0, t], seq=ahead))
                src = block(full, count, zb, core, cut if last else 0, count)
                moves.append(remote(src, src, ring_send.at[index, 1, t], ring_recv.at[index, 1, t], seq=behind))
            for move in moves:
                move.start()
            crossing = []
            for index, full, count, cut in arrays:
                src = block(full, count, zf, core)
                crossing.append(remote(src, src, cross_send.at[index, t], cross_recv.at[index, t], seq=other))
                if t > 0:
                    src = block(full, count, zb, core)
                    crossing.append(
                        remote(src, src, cross_send.at[index, steps + t], cross_recv.at[index, steps + t], seq=other)
                    )
            for move in crossing:
                move.start()
            if t == 0 and beside is not None:
                beside()
            for move in moves:
                move.wait_recv()
            sent += moves
            sent += crossing
        crossing = []
        for index, full, count, cut in arrays:
            src = block(full, count, (z + steps) % nz, core)
            crossing.append(remote(src, src, cross_send.at[index, steps], cross_recv.at[index, steps], seq=other))
        for move in crossing:
            move.start()
        for index, full, count, cut in arrays:
            for slot in range(2 * steps):
                src = block(full, count, z, core)
                remote(src, src, cross_send.at[index, slot], cross_recv.at[index, slot], seq=other).wait_recv()
        for move in sent + crossing:
            move.wait_send()

    def positions(shape, dim):
        return lax.broadcasted_iota(jnp.int32, shape, dim)

    def valid_rows(m, start, count):
        return (seq * frames + start + positions((count, 1), 0) < lengths[m]).astype(F32)

    def stem():
        for m in range(micro):
            for start in range(0, width, 256):
                value = jnp.dot(grouped[m], stem_full[:, start : start + 256], preferred_element_type=F32)
                value = value * jax.nn.sigmoid(value) * valid_rows(m, 0, frames)
                xs[micro + m, :, start : start + 256] = value.astype(BF16)

    @pl.when(first)
    def _():
        stem_keep.wait()
        stem_pair.wait()
        ring([(2, stem_full, 2 * stem_rows, stem_rows)])

    qkv_keep.wait()
    qkv_pair.wait()
    out_pair.wait()
    mine, theirs = out_in[...], out_peer[...]
    both = jnp.concatenate(
        [jnp.where(dp == 0, mine, theirs), jnp.where(dp == 0, theirs, mine)], axis=0
    )
    out_full[pl.ds(pl.multiple_of(seq * 2 * out_rows, 16), 2 * out_rows)] = both

    def beside():
        @pl.when(first)
        def _():
            stem()

    ring(
        [(0, qkv_full, 2 * qkv_rows, qkv_rows), (1, out_full, 2 * out_rows, (2 * out_rows) // 32 * 16 + 16 * ((2 * out_rows) // 16 % 2))],
        beside,
    )

    per_chunk = frames // CHUNKS

    def relay(m, c):
        start = c * per_chunk
        return remote(
            result.at[m, pl.ds(start, per_chunk)], xs.at[m, pl.ds(start, per_chunk)],
            relay_send.at[m, c], relay_recv.at[m, c], section=following,
        )

    def halo(m, part, side):
        columns = pl.ds(part * heads_width, heads_width)
        src = kv.at[m, pl.ds(frames, frames), columns]
        dst = kv.at[m, pl.ds(0 if side == 0 else 2 * frames, frames), columns]
        return remote(
            src, dst, halo_send.at[m, part, side], halo_recv.at[m, part, side], seq=right if side == 0 else left
        )

    def rim(m, side):
        src = conv_in.at[m, pl.ds(frames if side == 0 else 8, 8)]
        dst = conv_in.at[m, pl.ds(0 if side == 0 else 8 + frames, 8)]
        return remote(src, dst, rim_send.at[m, side], rim_recv.at[m, side], seq=right if side == 0 else left)

    def keep(m):
        return pltpu.make_async_copy(xs.at[m], arrivals.at[m], done_sem.at[m])

    def norm(value, gain):
        average = jnp.mean(value, axis=-1, keepdims=True)
        centered = value - average
        variance = jnp.mean(centered * centered, axis=-1, keepdims=True)
        return centered * lax.rsqrt(variance + eps) * gain

    def layer(m, carry):
        length = lengths[m]
        span = 3 * frames
        query = positions((frames, span), 0)
        key = positions((frames, span), 1)
        place = seq * frames - frames + key
        allowed = (place >= 0) & (place < length) & (key >= query) & (key <= query + 2 * frames)
        mask[...] = jnp.where(allowed, 0.0, masked_score).astype(F32)

        @pl.when(jnp.logical_not(first))
        def _():
            for c in range(CHUNKS):
                relay(m, c).wait_recv()
            keep(m).start()

        slot = jnp.where(first, micro + m, m)
        for start in range(0, frames, 16):
            value = xs[slot, start : start + 16, :].astype(F32)
            normed[start : start + 16, :] = norm(value, gains[0:1, :]).astype(BF16)

        for part in range(2):
            for start in range(0, heads_width, 256):
                at = heads_width * (1 + part) + start
                value = jnp.dot(normed[...], qkv_full[:, at : at + 256], preferred_element_type=F32)
                at = heads_width * part + start
                kv[m, frames : 2 * frames, at : at + 256] = value.astype(BF16)
            halo(m, part, 0).start()
            halo(m, part, 1).start()
        for start in range(0, heads_width, 256):
            value = jnp.dot(normed[...], qkv_full[:, start : start + 256], preferred_element_type=F32)
            queries[:, start : start + 256] = value.astype(BF16)
        for part in range(2):
            halo(m, part, 0).wait_recv()
            halo(m, part, 1).wait_recv()

        scale = 1.0 / head_size**0.5
        for group in range(HEADS // 4):
            base = group * 4 * head_size
            outs = []
            for h in range(4):
                low, high = h * head_size, (h + 1) * head_size
                lane_low, lane_high = low // 128 * 128, -(-high // 128) * 128
                lane = positions((frames, lane_high - lane_low), 1) + lane_low
                q = queries[:, base + lane_low : base + lane_high]
                q = jnp.where((lane >= low) & (lane < high), q, jnp.zeros_like(q))
                k = kv[m, :, base + lane_low : base + lane_high]
                v = kv[m, :, heads_width + base + lane_low : heads_width + base + lane_high]
                scores = lax.dot_general(q, k, (((1,), (1,)), ((), ())), preferred_element_type=F32)
                scores = scores * scale + mask[...]
                highest = jnp.max(scores, axis=-1, keepdims=True)
                expon = jnp.exp(scores - highest)
                total = jnp.sum(expon, axis=-1, keepdims=True)
                probs = (expon * (1.0 / total)).astype(BF16)
                outs.append(jnp.dot(probs, v, preferred_element_type=F32))
            lane = positions((frames, 128), 1)
            tiles = [
                jnp.where(lane < 96, outs[0], outs[1][:, :128]),
                jnp.where(lane < 64, outs[1][:, 128:], outs[2][:, :128]),
                jnp.where(lane < 32, outs[2][:, 128:], outs[3]),
            ]
            for index, tile in enumerate(tiles):
                at = base + index * 128
                context[:, at : at + 128] = tile.astype(BF16)

        for start in range(0, width, 256):
            value = jnp.dot(context[...], out_full[:, start : start + 256], preferred_element_type=F32)
            stream[:, start : start + 256] = value + xs[slot, :, start : start + 256].astype(F32)

        for start in range(0, frames, 16):
            value = norm(stream[start : start + 16, :], gains[1:2, :]) * valid_rows(m, start, 16)
            conv_in[m, 8 + start : 8 + start + 16, :] = value.astype(BF16).astype(F32)
        for side in range(2):
            rim(m, side).start()
        for side in range(2):
            rim(m, side).wait_recv()
        conv_in[m, 0:8, :] = jnp.where(seq == 0, 0.0, conv_in[m, 0:8, :])
        conv_in[m, 8 + frames : 16 + frames, :] = jnp.where(seq == nseq - 1, 0.0, conv_in[m, 8 + frames : 16 + frames, :])

        count = taps.shape[0]
        for c in range(CHUNKS):
            for start in range(c * per_chunk, (c + 1) * per_chunk, 16):
                conv = jnp.zeros((16, width), F32)
                for offset in range(count):
                    at = 8 - count // 2 + start + offset
                    conv = conv + conv_in[m, at : at + 16, :] * taps[offset : offset + 1, :]
                value = (stream[start : start + 16, :] + conv * jax.nn.sigmoid(conv)) * valid_rows(m, start, 16)
                result[m, start : start + 16, :] = value.astype(BF16)
            relay(m, c).start()
        return carry

    lax.fori_loop(0, micro, layer, 0)

    @pl.when(first)
    def _():
        for m in range(micro):
            for c in range(CHUNKS):
                relay(m, c).wait_recv()
            keep(m).start()

    for m in range(micro):
        for c in range(CHUNKS):
            relay(m, c).wait_send()
        for side in range(2):
            rim(m, side).wait_send()
            for part in range(2):
                halo(m, part, side).wait_send()
        keep(m).wait()


def shards(sections, nseq, mel, lengths, stem_weight, w_qkv, w_out, norm_gains, conv_kernel):
    micro = mel.shape[0]
    frames = mel.shape[1] // STRIDE
    width = stem_weight.shape[1]
    heads_width = w_qkv.shape[2] // 3
    grouped = mel.reshape(micro, frames, STRIDE * mel.shape[2])
    depth, full_out = w_qkv.shape[1] * 2 * nseq, w_out.shape[1] * 2 * nseq
    steps = nseq // 4
    dma = pltpu.SemaphoreType.DMA
    vmem = pl.BlockSpec(memory_space=pltpu.VMEM)
    arrived = pl.pallas_call(
        functools.partial(kernel, sections, nseq),
        out_shape=jax.ShapeDtypeStruct((micro, frames, width), BF16),
        in_specs=[pl.BlockSpec(memory_space=pltpu.SMEM)] + [vmem] * 6,
        out_specs=pl.BlockSpec(memory_space=pl.ANY),
        scratch_shapes=[
            pltpu.VMEM((stem_weight.shape[0] * 2 * nseq, width), BF16),
            pltpu.VMEM((depth, 3 * heads_width), BF16),
            pltpu.VMEM((full_out, width), BF16),
            pltpu.VMEM(w_out.shape[1:], BF16),
            pltpu.VMEM((2 * micro, frames, width), BF16),
            pltpu.VMEM((frames, width), BF16),
            pltpu.VMEM((micro, 3 * frames, 2 * heads_width), BF16),
            pltpu.VMEM((frames, heads_width), BF16),
            pltpu.VMEM((frames, heads_width), BF16),
            pltpu.VMEM((frames, 3 * frames), F32),
            pltpu.VMEM((frames, width), F32),
            pltpu.VMEM((micro, frames + 16, width), F32),
            pltpu.VMEM((micro, frames, width), BF16),
            dma((2,)),
            dma((3,)),
            dma((3,)),
            dma((3, 2, steps)),
            dma((3, 2, steps)),
            dma((3, 2 * steps)),
            dma((3, 2 * steps)),
            dma((micro, 2, 2)),
            dma((micro, 2, 2)),
            dma((micro, 2)),
            dma((micro, 2)),
            dma((micro, CHUNKS)),
            dma((micro, CHUNKS)),
            dma((micro,)),
        ],
        compiler_params=pltpu.CompilerParams(
            collective_id=0, has_side_effects=True, vmem_limit_bytes=48 * 1024 * 1024
        ),
    )(lengths, grouped, stem_weight, w_qkv[0], w_out[0], norm_gains[0], conv_kernel[0])
    return arrived[None]


def solution(mesh):
    return jax.shard_map(
        functools.partial(shards, mesh.shape["section"], mesh.shape["seq"]),
        mesh=mesh,
        in_specs=(
            P("dp", "seq", None),
            P("dp"),
            P(("seq", "dp"), None),
            P("section", ("seq", "dp"), None),
            P("section", ("seq", "dp"), None),
            P("section", None, None),
            P("section", None, None),
        ),
        out_specs=P("section", "dp", "seq", None),
        check_vma=False,
    )
```

```python
import functools

import jax
import jax.numpy as jnp
from jax import lax
from jax.experimental import pallas as pl
from jax.experimental.pallas import tpu as pltpu
from jax.sharding import PartitionSpec as P

HEADS = 8
STRIDE = 4
eps = 1e-05
masked_score = -1e30
F32 = jnp.float32
BF16 = jnp.bfloat16
MESH = pl.DeviceIdType.MESH


def remote(src, dst, send, recv, **device):
    return pltpu.make_async_remote_copy(
        src_ref=src, dst_ref=dst, send_sem=send, recv_sem=recv, device_id=device, device_id_type=MESH
    )


def rows(ref, start, count):
    return ref.at[pl.ds(pl.multiple_of(start, 16), count)]


def kernel(
    sections, nseq,
    lengths, grouped, stem_in, qkv_in, out_in, gains, taps, arrivals,
    stem_full, qkv_full, out_full, out_peer, xs, normed, kv, queries, context, mask, stream, conv_in, result,
    local_sem, pair_send, pair_recv, ring_send, ring_recv, cross_send, cross_recv,
    halo_send, halo_recv, rim_send, rim_recv, relay_send, relay_recv, done_sem,
):
    section = lax.axis_index("section")
    seq = lax.axis_index("seq")
    dp = lax.axis_index("dp")
    nz = nseq // 2
    z, core = lax.div(seq, 2), lax.rem(seq, 2)
    ahead = lax.rem(z + 1, nz) * 2 + core
    behind = lax.rem(z + nz - 1, nz) * 2 + core
    other = seq + 1 - 2 * core
    right, left = lax.rem(seq + 1, nseq), lax.rem(seq + nseq - 1, nseq)
    far = jnp.where(core == 1, right, left)
    following, preceding = lax.rem(section + 1, sections), lax.rem(section + sections - 1, sections)
    first = section == 0

    micro, frames, width = xs.shape[0] // 2, xs.shape[1], xs.shape[2]
    heads_width = queries.shape[1]
    head_size = heads_width // HEADS
    stem_rows, qkv_rows, out_rows = stem_in.shape[0], qkv_in.shape[0], out_in.shape[0]

    barrier = pltpu.get_barrier_semaphore()
    for device in (
        {"seq": ahead}, {"seq": behind}, {"seq": other}, {"seq": far},
        {"dp": 1 - dp}, {"section": following}, {"section": preceding},
    ):
        pl.semaphore_signal(barrier, inc=1, device_id=device, device_id_type=MESH)
    pl.semaphore_wait(barrier, 7)

    def own_rows(full, count):
        return rows(full, (seq * 2 + dp) * count, count)

    stem_pair = remote(stem_in, own_rows(stem_full, stem_rows), pair_send.at[2], pair_recv.at[2], dp=1 - dp)
    stem_keep = pltpu.make_async_copy(stem_in, own_rows(stem_full, stem_rows), local_sem.at[1])
    qkv_pair = remote(qkv_in, own_rows(qkv_full, qkv_rows), pair_send.at[0], pair_recv.at[0], dp=1 - dp)
    qkv_keep = pltpu.make_async_copy(qkv_in, own_rows(qkv_full, qkv_rows), local_sem.at[0])
    out_pair = remote(out_in, out_peer, pair_send.at[1], pair_recv.at[1], dp=1 - dp)

    @pl.when(first)
    def _():
        stem_pair.start()
        stem_keep.start()

    qkv_pair.start()
    qkv_keep.start()
    out_pair.start()

    steps = nz // 2

    places = [
        [(lax.rem(z + nz - t, nz) * 2 + core) for t in range(steps + 1)],
        [(lax.rem(z + t, nz) * 2 + core) for t in range(steps)],
    ]
    out_cut = -(-out_rows // 16) * 16
    arrays = {
        "stem": (0, stem_full, stem_rows, 0, 2 * stem_rows, stem_rows),
        "own": (1, qkv_full, qkv_rows, dp * qkv_rows, qkv_rows, qkv_rows),
        "peer": (2, qkv_full, qkv_rows, (1 - dp) * qkv_rows, qkv_rows, 0),
        "out": (3, out_full, out_rows, 0, 2 * out_rows, out_cut),
    }
    hops, crosses = {}, {}
    for name, (index, full, count, low, size, cut) in arrays.items():
        for side in range(2):
            for t in range(steps):
                start, length = places[side][t] * (2 * count) + low, size
                if t == steps - 1:
                    start, length = (start, cut) if side == 0 else (start + cut, size - cut)
                if length:
                    src = rows(full, start, length)
                    hops[name, side, t] = remote(
                        src, src, ring_send.at[index, side, t], ring_recv.at[index, side, t],
                        seq=ahead if side == 0 else behind,
                    )
        for slot in range(2 * steps):
            place = places[0][slot] if slot <= steps else places[1][slot - steps]
            src = rows(full, place * (2 * count) + low, size)
            crosses[name, slot] = remote(src, src, cross_send.at[index, slot], cross_recv.at[index, slot], seq=other)

    def hop(name, side, t):
        return hops.get((name, side, t))

    def cross(name, slot):
        return crosses[name, slot]

    def ring_open(name):
        for side in range(2):
            hop(name, side, 0).start()
        cross(name, 0).start()

    def ring_step(name, t):
        for side in range(2):
            hop(name, side, t - 1).wait_recv()
            move = hop(name, side, t)
            if move is not None:
                move.start()
            cross(name, t if side == 0 else steps + t).start()

    def ring_close(name):
        for side in range(2):
            move = hop(name, side, steps - 1)
            if move is not None:
                move.wait_recv()
        cross(name, steps).start()
        for slot in range(2 * steps):
            cross(name, slot).wait_recv()

    def ring_sent(name):
        for t in range(steps):
            for side in range(2):
                move = hop(name, side, t)
                if move is not None:
                    move.wait_send()
        for slot in range(2 * steps):
            cross(name, slot).wait_send()

    def positions(shape, dim):
        return lax.broadcasted_iota(jnp.int32, shape, dim)

    def valid_rows(m, start, count):
        return jnp.where(positions((count, 1), 0) < lengths[m] - seq * frames - start, 1.0, 0.0)

    def stem():
        for m in range(micro):
            for start in range(0, width, 256):
                value = jnp.dot(grouped[m], stem_full[:, start : start + 256], preferred_element_type=F32)
                value = value * jax.nn.sigmoid(value) * valid_rows(m, 0, frames)
                xs[micro + m, :, start : start + 256] = value.astype(BF16)

    qkv_keep.wait()
    ring_open("own")

    @pl.when(first)
    def _():
        stem_keep.wait()
        stem_pair.wait()
        ring_open("stem")

    qkv_pair.wait()
    ring_open("peer")
    out_pair.wait()
    mine, theirs = out_in[...], out_peer[...]
    both = jnp.concatenate(
        [jnp.where(dp == 0, mine, theirs), jnp.where(dp == 0, theirs, mine)], axis=0
    )
    out_full[pl.ds(pl.multiple_of(seq * 2 * out_rows, 16), 2 * out_rows)] = both
    ring_open("out")
    for t in range(1, steps):
        @pl.when(first)
        def _():
            ring_step("stem", t)

        for name in ("own", "peer", "out"):
            ring_step(name, t)

    @pl.when(first)
    def _():
        ring_close("stem")
        stem()
        ring_sent("stem")

    ring_close("own")
    ring_close("peer")

    units = ((16, frames // 2 - 16), (frames // 2, frames // 2 - 16), (0, 16), (frames - 16, 16))
    groups = ((0,), (1,), (2, 3))

    def relay(m, unit):
        start, count = units[unit]
        return remote(
            result.at[m, pl.ds(start, count)], xs.at[m, pl.ds(start, count)],
            relay_send.at[m, unit], relay_recv.at[m, unit], section=following,
        )

    def halo(m, unit, side):
        start, count = units[unit]
        src = kv.at[m, pl.ds(frames + start, count)]
        dst = kv.at[m, pl.ds(start if side == 0 else 2 * frames + start, count)]
        return remote(
            src, dst, halo_send.at[m, unit, side], halo_recv.at[m, unit, side], seq=right if side == 0 else left
        )

    def rim(m, side):
        src = conv_in.at[m, pl.ds(frames if side == 0 else 8, 8)]
        dst = conv_in.at[m, pl.ds(0 if side == 0 else 8 + frames, 8)]
        return remote(src, dst, rim_send.at[m, side], rim_recv.at[m, side], seq=right if side == 0 else left)

    def keep(m):
        return pltpu.make_async_copy(xs.at[m], arrivals.at[m], done_sem.at[m])

    def norm(value, gain):
        average = jnp.mean(value, axis=-1, keepdims=True)
        centered = value - average
        variance = jnp.mean(centered * centered, axis=-1, keepdims=True)
        return centered * lax.rsqrt(variance + eps) * gain

    def layer(m, carry):
        length = lengths[m]
        span = 3 * frames
        query = positions((frames, span), 0)
        key = positions((frames, span), 1)
        place = seq * frames - frames + key
        allowed = (place >= 0) & (place < length) & (key >= query) & (key <= query + 2 * frames)
        mask[...] = jnp.where(allowed, 0.0, masked_score).astype(F32)

        slot = jnp.where(first, micro + m, m)
        for group in groups:
            @pl.when(jnp.logical_not(first))
            def _():
                for unit in group:
                    relay(m, unit).wait_recv()

            for unit in group:
                for start in range(units[unit][0], sum(units[unit]), 16):
                    value = xs[slot, start : start + 16, :].astype(F32)
                    normed[start : start + 16, :] = norm(value, gains[0:1, :]).astype(BF16)
            some = [normed[units[unit][0] : sum(units[unit]), :] for unit in group]
            some = some[0] if len(some) == 1 else jnp.concatenate(some, axis=0)
            for start in range(0, 2 * heads_width, 256):
                at = heads_width + start
                value = jnp.dot(some, qkv_full[:, at : at + 256], preferred_element_type=F32).astype(BF16)
                low = 0
                for unit in group:
                    at, count = units[unit]
                    kv[m, frames + at : frames + at + count, start : start + 256] = value[low : low + count]
                    low += count
            for unit in group:
                for side in range(2):
                    halo(m, unit, side).start()

        @pl.when(jnp.logical_not(first))
        def _():
            keep(m).start()

        for start in range(0, heads_width, 256):
            value = jnp.dot(normed[...], qkv_full[:, start : start + 256], preferred_element_type=F32)
            queries[:, start : start + 256] = value.astype(BF16)
        for unit in range(len(units)):
            for side in range(2):
                halo(m, unit, side).wait_recv()

        scale = 1.0 / head_size**0.5
        for group in range(HEADS // 4):
            base = group * 4 * head_size
            outs = []
            for h in range(4):
                low, high = h * head_size, (h + 1) * head_size
                lane_low, lane_high = low // 128 * 128, -(-high // 128) * 128
                lane = positions((frames, lane_high - lane_low), 1) + lane_low
                q = queries[:, base + lane_low : base + lane_high]
                q = jnp.where((lane >= low) & (lane < high), q, jnp.zeros_like(q))
                k = kv[m, :, base + lane_low : base + lane_high]
                v = kv[m, :, heads_width + base + lane_low : heads_width + base + lane_high]
                scores = lax.dot_general(q, k, (((1,), (1,)), ((), ())), preferred_element_type=F32)
                scores = scores * scale + mask[...]
                highest = jnp.max(scores, axis=-1, keepdims=True)
                expon = jnp.exp(scores - highest)
                total = jnp.sum(expon, axis=-1, keepdims=True)
                probs = (expon * (1.0 / total)).astype(BF16)
                outs.append(jnp.dot(probs, v, preferred_element_type=F32))
            lane = positions((frames, 128), 1)
            tiles = [
                jnp.where(lane < 96, outs[0], outs[1][:, :128]),
                jnp.where(lane < 64, outs[1][:, 128:], outs[2][:, :128]),
                jnp.where(lane < 32, outs[2][:, 128:], outs[3]),
            ]
            for index, tile in enumerate(tiles):
                at = base + index * 128
                context[:, at : at + 128] = tile.astype(BF16)

        @pl.when(m == 0)
        def _():
            ring_close("out")

        for start in range(0, width, 256):
            value = jnp.dot(context[...], out_full[:, start : start + 256], preferred_element_type=F32)
            stream[:, start : start + 256] = value + xs[slot, :, start : start + 256].astype(F32)

        for start in range(0, frames, 16):
            value = norm(stream[start : start + 16, :], gains[1:2, :]) * valid_rows(m, start, 16)
            conv_in[m, 8 + start : 8 + start + 16, :] = value.astype(BF16).astype(F32)
        for side in range(2):
            rim(m, side).start()
        count = taps.shape[0]
        for unit in range(len(units)):
            if unit == 2:
                for side in range(2):
                    rim(m, side).wait_recv()
                top, bottom = conv_in[m, 0:8, :], conv_in[m, 8 + frames : 16 + frames, :]
                conv_in[m, 0:8, :] = jnp.where(seq == 0, 0.0, top)
                conv_in[m, 8 + frames : 16 + frames, :] = jnp.where(seq == nseq - 1, 0.0, bottom)
            for start in range(units[unit][0], sum(units[unit]), 16):
                conv = jnp.zeros((16, width), F32)
                for offset in range(count):
                    at = 8 - count // 2 + start + offset
                    conv = conv + conv_in[m, at : at + 16, :] * taps[offset : offset + 1, :]
                value = (stream[start : start + 16, :] + conv * jax.nn.sigmoid(conv)) * valid_rows(m, start, 16)
                result[m, start : start + 16, :] = value.astype(BF16)
            relay(m, unit).start()
        return carry

    lax.fori_loop(0, micro, layer, 0)

    @pl.when(first)
    def _():
        for m in range(micro):
            for unit in range(len(units)):
                relay(m, unit).wait_recv()
            keep(m).start()

    for name in ("own", "peer", "out"):
        ring_sent(name)
    for m in range(micro):
        for unit in range(len(units)):
            relay(m, unit).wait_send()
            for side in range(2):
                halo(m, unit, side).wait_send()
        for side in range(2):
            rim(m, side).wait_send()
        keep(m).wait()


def shards(sections, nseq, mel, lengths, stem_weight, w_qkv, w_out, norm_gains, conv_kernel):
    micro = mel.shape[0]
    frames = mel.shape[1] // STRIDE
    width = stem_weight.shape[1]
    heads_width = w_qkv.shape[2] // 3
    grouped = mel.reshape(micro, frames, STRIDE * mel.shape[2])
    depth, full_out = w_qkv.shape[1] * 2 * nseq, w_out.shape[1] * 2 * nseq
    steps = nseq // 4
    dma = pltpu.SemaphoreType.DMA
    vmem = pl.BlockSpec(memory_space=pltpu.VMEM)
    arrived = pl.pallas_call(
        functools.partial(kernel, sections, nseq),
        out_shape=jax.ShapeDtypeStruct((micro, frames, width), BF16),
        in_specs=[pl.BlockSpec(memory_space=pltpu.SMEM)] + [vmem] * 6,
        out_specs=pl.BlockSpec(memory_space=pl.ANY),
        scratch_shapes=[
            pltpu.VMEM((stem_weight.shape[0] * 2 * nseq, width), BF16),
            pltpu.VMEM((depth, 3 * heads_width), BF16),
            pltpu.VMEM((full_out, width), BF16),
            pltpu.VMEM(w_out.shape[1:], BF16),
            pltpu.VMEM((2 * micro, frames, width), BF16),
            pltpu.VMEM((frames, width), BF16),
            pltpu.VMEM((micro, 3 * frames, 2 * heads_width), BF16),
            pltpu.VMEM((frames, heads_width), BF16),
            pltpu.VMEM((frames, heads_width), BF16),
            pltpu.VMEM((frames, 3 * frames), F32),
            pltpu.VMEM((frames, width), F32),
            pltpu.VMEM((micro, frames + 16, width), F32),
            pltpu.VMEM((micro, frames, width), BF16),
            dma((2,)),
            dma((3,)),
            dma((3,)),
            dma((4, 2, steps)),
            dma((4, 2, steps)),
            dma((4, 2 * steps)),
            dma((4, 2 * steps)),
            dma((micro, 4, 2)),
            dma((micro, 4, 2)),
            dma((micro, 2)),
            dma((micro, 2)),
            dma((micro, 4)),
            dma((micro, 4)),
            dma((micro,)),
        ],
        compiler_params=pltpu.CompilerParams(
            collective_id=0, has_side_effects=True, vmem_limit_bytes=48 * 1024 * 1024
        ),
    )(lengths, grouped, stem_weight, w_qkv[0], w_out[0], norm_gains[0], conv_kernel[0])
    return arrived[None]


def solution(mesh):
    return jax.shard_map(
        functools.partial(shards, mesh.shape["section"], mesh.shape["seq"]),
        mesh=mesh,
        in_specs=(
            P("dp", "seq", None),
            P("dp"),
            P(("seq", "dp"), None),
            P("section", ("seq", "dp"), None),
            P("section", ("seq", "dp"), None),
            P("section", None, None),
            P("section", None, None),
        ),
        out_specs=P("section", "dp", "seq", None),
        check_vma=False,
    )
```

```python
import functools

import jax
import jax.numpy as jnp
from jax import lax
from jax.experimental import pallas as pl
from jax.experimental.pallas import tpu as pltpu
from jax.sharding import PartitionSpec as P

HEADS = 8
STRIDE = 4
eps = 1e-05
masked_score = -1e30
F32 = jnp.float32
BF16 = jnp.bfloat16
MESH = pl.DeviceIdType.MESH


def remote(src, dst, send, recv, **device):
    return pltpu.make_async_remote_copy(
        src_ref=src, dst_ref=dst, send_sem=send, recv_sem=recv, device_id=device, device_id_type=MESH
    )


def rows(ref, start, count):
    return ref.at[pl.ds(pl.multiple_of(start, 16), count)]


def kernel(
    sections, nseq,
    lengths, grouped, stem_in, qkv_in, out_in, gains, taps, arrivals,
    stem_full, qkv_full, out_full, out_peer, xs, normed, kv, queries, context, mask, scores, stream, conv_in, result,
    local_sem, pair_send, pair_recv, ring_send, ring_recv, cross_send, cross_recv, pass_send, pass_recv,
    halo_send, halo_recv, rim_send, rim_recv, relay_send, relay_recv, done_sem,
):
    section = lax.axis_index("section")
    seq = lax.axis_index("seq")
    dp = lax.axis_index("dp")
    nz = nseq // 2
    z, core = lax.div(seq, 2), lax.rem(seq, 2)
    ahead = lax.rem(z + 1, nz) * 2 + core
    behind = lax.rem(z + nz - 1, nz) * 2 + core
    other = seq + 1 - 2 * core
    right, left = lax.rem(seq + 1, nseq), lax.rem(seq + nseq - 1, nseq)
    far = jnp.where(core == 1, right, left)
    following, preceding = lax.rem(section + 1, sections), lax.rem(section + sections - 1, sections)
    first = section == 0

    micro, frames, width = xs.shape[0] // 2, xs.shape[1], xs.shape[2]
    heads_width = queries.shape[1]
    head_size = heads_width // HEADS
    stem_rows, qkv_rows, out_rows = stem_in.shape[0], qkv_in.shape[0], out_in.shape[0]

    barrier = pltpu.get_barrier_semaphore()
    for device in (
        {"seq": ahead}, {"seq": behind}, {"seq": other}, {"seq": far},
        {"dp": 1 - dp}, {"section": following}, {"section": preceding},
    ):
        pl.semaphore_signal(barrier, inc=1, device_id=device, device_id_type=MESH)
    pl.semaphore_wait(barrier, 7)

    def own_rows(full, count):
        return rows(full, (seq * 2 + dp) * count, count)

    stem_pair = remote(stem_in, own_rows(stem_full, stem_rows), pair_send.at[2], pair_recv.at[2], dp=1 - dp)
    stem_keep = pltpu.make_async_copy(stem_in, own_rows(stem_full, stem_rows), local_sem.at[1])
    qkv_pair = remote(qkv_in, own_rows(qkv_full, qkv_rows), pair_send.at[0], pair_recv.at[0], dp=1 - dp)
    qkv_keep = pltpu.make_async_copy(qkv_in, own_rows(qkv_full, qkv_rows), local_sem.at[0])
    out_pair = remote(out_in, out_peer, pair_send.at[1], pair_recv.at[1], dp=1 - dp)

    @pl.when(first)
    def _():
        stem_pair.start()
        stem_keep.start()

    qkv_pair.start()
    qkv_keep.start()
    out_pair.start()

    steps = nz // 2

    places = [
        [(lax.rem(z + nz - t, nz) * 2 + core) for t in range(steps + 1)],
        [(lax.rem(z + t, nz) * 2 + core) for t in range(steps)],
    ]
    out_cut = out_rows // 16 * 16
    arrays = {
        "stem": (0, stem_full, stem_rows, 0, 2 * stem_rows, stem_rows),
        "own": (1, qkv_full, qkv_rows, dp * qkv_rows, qkv_rows, qkv_rows),
        "peer": (2, qkv_full, qkv_rows, (1 - dp) * qkv_rows, qkv_rows, qkv_rows),
        "out": (3, out_full, out_rows, 0, 2 * out_rows, out_cut),
    }
    hops, crosses, pairs = {}, {}, {}
    for name, (index, full, count, low, size, cut) in arrays.items():
        for side in range(2):
            for t in range(1 if name == "peer" else steps):
                start, length = places[side][t] * (2 * count) + low, size
                if t == steps - 1:
                    start, length = (start, cut) if side == 0 else (start + cut, size - cut)
                if length:
                    src = rows(full, start, length)
                    hops[name, side, t] = remote(
                        src, src, ring_send.at[index, side, t], ring_recv.at[index, side, t],
                        seq=ahead if side == 0 else behind,
                    )
        for slot in range(2 * steps):
            place = places[0][slot] if slot <= steps else places[1][slot - steps]
            src = rows(full, place * (2 * count) + low, size)
            crosses[name, slot] = remote(src, src, cross_send.at[index, slot], cross_recv.at[index, slot], seq=other)
            if name == "own" and slot not in (0, 1, steps + 1):
                pairs[slot] = remote(src, src, pass_send.at[slot], pass_recv.at[slot], dp=1 - dp)

    def hop(name, side, t):
        return hops.get((name, side, t))

    def cross(name, slot):
        return crosses[name, slot]

    def ring_open(name):
        for side in range(2):
            hop(name, side, 0).start()
        cross(name, 0).start()

    def ring_step(name, t):
        for side in range(2):
            slot = t if side == 0 else steps + t
            hop(name, side, t - 1).wait_recv()
            move = hop(name, side, t)
            if move is not None:
                move.start()
            cross(name, slot).start()
            if name == "own" and slot in pairs:
                pairs[slot].start()

    def ring_close(name):
        for side in range(2):
            move = hop(name, side, steps - 1)
            if move is not None:
                move.wait_recv()
        if name == "own":
            pairs[steps].start()
        if name != "peer":
            cross(name, steps).start()
        for slot in range(2 * steps):
            if name == "peer" and slot in pairs:
                pairs[slot].wait_recv()
                cross(name, slot).start()
        for slot in range(2 * steps):
            cross(name, slot).wait_recv()

    def ring_sent(name):
        for t in range(steps):
            for side in range(2):
                move = hop(name, side, t)
                if move is not None:
                    move.wait_send()
        for slot in range(2 * steps):
            cross(name, slot).wait_send()
            if name == "own" and slot in pairs:
                pairs[slot].wait_send()

    def positions(shape, dim):
        return lax.broadcasted_iota(jnp.int32, shape, dim)

    def valid_rows(m, start, count):
        return jnp.where(positions((count, 1), 0) < lengths[m] - seq * frames - start, 1.0, 0.0)

    def stem():
        for m in range(micro):
            for start in range(0, width, 256):
                value = jnp.dot(grouped[m], stem_full[:, start : start + 256], preferred_element_type=F32)
                value = value * jax.nn.sigmoid(value) * valid_rows(m, 0, frames)
                xs[micro + m, :, start : start + 256] = value.astype(BF16)

    qkv_keep.wait()
    ring_open("own")

    @pl.when(first)
    def _():
        stem_keep.wait()
        stem_pair.wait()
        ring_open("stem")

    qkv_pair.wait()
    ring_open("peer")
    out_pair.wait()
    mine, theirs = out_in[...], out_peer[...]
    both = jnp.concatenate(
        [jnp.where(dp == 0, mine, theirs), jnp.where(dp == 0, theirs, mine)], axis=0
    )
    out_full[pl.ds(pl.multiple_of(seq * 2 * out_rows, 16), 2 * out_rows)] = both
    ring_open("out")
    for t in range(1, steps):
        @pl.when(first)
        def _():
            ring_step("stem", t)

        for name in ("own", "peer", "out") if t == 1 else ("own", "out"):
            ring_step(name, t)

    @pl.when(first)
    def _():
        ring_close("stem")
        stem()
        ring_sent("stem")

    ring_close("own")
    ring_close("peer")

    units = ((16, frames // 2 - 16), (frames // 2, frames // 2 - 16), (0, 16), (frames - 16, 16))
    groups = ((0,), (1,), (2, 3))

    def relay(m, unit):
        start, count = units[unit]
        return remote(
            result.at[m, pl.ds(start, count)], xs.at[m, pl.ds(start, count)],
            relay_send.at[m, unit], relay_recv.at[m, unit], section=following,
        )

    def halo(m, unit, side):
        start, count = units[unit]
        src = kv.at[m, pl.ds(frames + start, count)]
        dst = kv.at[m, pl.ds(2 * frames * side + start, count)]
        return remote(
            src, dst, halo_send.at[m, unit, side], halo_recv.at[m, unit, side], seq=right if side == 0 else left
        )

    near_side, far_side = 1 - core, core
    near_keys = pl.multiple_of(frames * (1 - core), 128)
    far_keys = pl.multiple_of(2 * frames * core, 128)

    def halo_wait(m, side):
        for unit, (start, count) in enumerate(units):
            src = kv.at[m, pl.ds(frames + start, count)]
            dst = rows(kv.at[m], 2 * frames * side + start, count)
            remote(src, dst, halo_send.at[m, unit, side], halo_recv.at[m, unit, side], seq=right).wait_recv()

    def rim(m, side):
        src = conv_in.at[m, pl.ds(frames if side == 0 else 8, 8)]
        dst = conv_in.at[m, pl.ds(0 if side == 0 else 8 + frames, 8)]
        return remote(src, dst, rim_send.at[m, side], rim_recv.at[m, side], seq=right if side == 0 else left)

    def keep(m):
        return pltpu.make_async_copy(xs.at[m], arrivals.at[m], done_sem.at[m])

    def norm(value, gain):
        average = jnp.mean(value, axis=-1, keepdims=True)
        centered = value - average
        variance = jnp.mean(centered * centered, axis=-1, keepdims=True)
        return centered * lax.rsqrt(variance + eps) * gain

    def layer(m, carry):
        length = lengths[m]
        span = 3 * frames
        query = positions((frames, span), 0)
        column = positions((frames, span), 1)
        key = jnp.where(column < 2 * frames, column + near_keys, column + (far_keys - 2 * frames))
        place = seq * frames - frames + key
        allowed = (place >= 0) & (place < length) & (key >= query) & (key <= query + 2 * frames)
        mask[...] = jnp.where(allowed, 0.0, masked_score).astype(F32)

        slot = jnp.where(first, micro + m, m)
        for group in groups:
            @pl.when(jnp.logical_not(first))
            def _():
                for unit in group:
                    relay(m, unit).wait_recv()

            for unit in group:
                for start in range(units[unit][0], sum(units[unit]), 16):
                    value = xs[slot, start : start + 16, :].astype(F32)
                    normed[start : start + 16, :] = norm(value, gains[0:1, :]).astype(BF16)
            some = [normed[units[unit][0] : sum(units[unit]), :] for unit in group]
            some = some[0] if len(some) == 1 else jnp.concatenate(some, axis=0)
            for start in range(0, 2 * heads_width, 256):
                at = heads_width + start
                value = jnp.dot(some, qkv_full[:, at : at + 256], preferred_element_type=F32).astype(BF16)
                low = 0
                for unit in group:
                    at, count = units[unit]
                    kv[m, frames + at : frames + at + count, start : start + 256] = value[low : low + count]
                    low += count
            for unit in group:
                for side in range(2):
                    halo(m, unit, side).start()

        @pl.when(jnp.logical_not(first))
        def _():
            keep(m).start()

        for start in range(0, heads_width, 256):
            value = jnp.dot(normed[...], qkv_full[:, start : start + 256], preferred_element_type=F32)
            queries[:, start : start + 256] = value.astype(BF16)
        windows = []
        for h in range(HEADS):
            base, low = h // 4 * 4 * head_size, h % 4 * head_size
            windows.append((base, low, low + head_size, low // 128 * 128, -(-(low + head_size) // 128) * 128))

        def score(first_key, count, at):
            for h, (base, low, high, lane_low, lane_high) in enumerate(windows):
                lane = positions((frames, lane_high - lane_low), 1) + lane_low
                q = queries[:, base + lane_low : base + lane_high]
                q = jnp.where((lane >= low) & (lane < high), q, jnp.zeros_like(q))
                k = kv[m, pl.ds(first_key, count), base + lane_low : base + lane_high]
                scores[h, :, at : at + count] = lax.dot_general(
                    q, k, (((1,), (1,)), ((), ())), preferred_element_type=F32
                )

        halo_wait(m, near_side)
        score(near_keys, 2 * frames, 0)
        halo_wait(m, far_side)
        score(far_keys, frames, 2 * frames)

        scale = 1.0 / head_size**0.5
        lane = positions((frames, 128), 1)
        for group in range(HEADS // 4):
            outs = []
            for h in range(4 * group, 4 * group + 4):
                base, low, high, lane_low, lane_high = windows[h]
                columns = slice(heads_width + base + lane_low, heads_width + base + lane_high)
                value = scores[h] * scale + mask[...]
                expon = jnp.exp(value - jnp.max(value, axis=-1, keepdims=True))
                total = jnp.sum(expon, axis=-1, keepdims=True)
                probs = expon.astype(BF16)
                value = jnp.dot(
                    probs[:, : 2 * frames], kv[m, pl.ds(near_keys, 2 * frames), columns], preferred_element_type=F32
                ) + jnp.dot(
                    probs[:, 2 * frames :], kv[m, pl.ds(far_keys, frames), columns], preferred_element_type=F32
                )
                outs.append(value * (1.0 / total))
            tiles = [
                jnp.where(lane < 96, outs[0], outs[1][:, :128]),
                jnp.where(lane < 64, outs[1][:, 128:], outs[2][:, :128]),
                jnp.where(lane < 32, outs[2][:, 128:], outs[3]),
            ]
            for index, tile in enumerate(tiles):
                at = 4 * head_size * group + index * 128
                context[:, at : at + 128] = tile.astype(BF16)

        @pl.when(m == 0)
        def _():
            ring_close("out")

        for start in range(0, width, 256):
            value = jnp.dot(context[...], out_full[:, start : start + 256], preferred_element_type=F32)
            stream[:, start : start + 256] = value + xs[slot, :, start : start + 256].astype(F32)

        for start in range(0, frames, 16):
            value = norm(stream[start : start + 16, :], gains[1:2, :]) * valid_rows(m, start, 16)
            conv_in[m, 8 + start : 8 + start + 16, :] = value.astype(BF16).astype(F32)
        for side in range(2):
            rim(m, side).start()
        count = taps.shape[0]
        for unit in range(len(units)):
            if unit == 2:
                for side in range(2):
                    rim(m, side).wait_recv()
                top, bottom = conv_in[m, 0:8, :], conv_in[m, 8 + frames : 16 + frames, :]
                conv_in[m, 0:8, :] = jnp.where(seq == 0, 0.0, top)
                conv_in[m, 8 + frames : 16 + frames, :] = jnp.where(seq == nseq - 1, 0.0, bottom)
            for start in range(units[unit][0], sum(units[unit]), 16):
                conv = jnp.zeros((16, width), F32)
                for offset in range(count):
                    at = 8 - count // 2 + start + offset
                    conv = conv + conv_in[m, at : at + 16, :] * taps[offset : offset + 1, :]
                value = (stream[start : start + 16, :] + conv * jax.nn.sigmoid(conv)) * valid_rows(m, start, 16)
                result[m, start : start + 16, :] = value.astype(BF16)
            relay(m, unit).start()
        return carry

    lax.fori_loop(0, micro, layer, 0)

    @pl.when(first)
    def _():
        for m in range(micro):
            for unit in range(len(units)):
                relay(m, unit).wait_recv()
            keep(m).start()

    for name in ("own", "peer", "out"):
        ring_sent(name)
    for m in range(micro):
        for unit in range(len(units)):
            relay(m, unit).wait_send()
            for side in range(2):
                halo(m, unit, side).wait_send()
        for side in range(2):
            rim(m, side).wait_send()
        keep(m).wait()


def shards(sections, nseq, mel, lengths, stem_weight, w_qkv, w_out, norm_gains, conv_kernel):
    micro = mel.shape[0]
    frames = mel.shape[1] // STRIDE
    width = stem_weight.shape[1]
    heads_width = w_qkv.shape[2] // 3
    grouped = mel.reshape(micro, frames, STRIDE * mel.shape[2])
    depth, full_out = w_qkv.shape[1] * 2 * nseq, w_out.shape[1] * 2 * nseq
    steps = nseq // 4
    dma = pltpu.SemaphoreType.DMA
    vmem = pl.BlockSpec(memory_space=pltpu.VMEM)
    arrived = pl.pallas_call(
        functools.partial(kernel, sections, nseq),
        out_shape=jax.ShapeDtypeStruct((micro, frames, width), BF16),
        in_specs=[pl.BlockSpec(memory_space=pltpu.SMEM)] + [vmem] * 6,
        out_specs=pl.BlockSpec(memory_space=pl.ANY),
        scratch_shapes=[
            pltpu.VMEM((stem_weight.shape[0] * 2 * nseq, width), BF16),
            pltpu.VMEM((depth, 3 * heads_width), BF16),
            pltpu.VMEM((full_out, width), BF16),
            pltpu.VMEM(w_out.shape[1:], BF16),
            pltpu.VMEM((2 * micro, frames, width), BF16),
            pltpu.VMEM((frames, width), BF16),
            pltpu.VMEM((micro, 3 * frames, 2 * heads_width), BF16),
            pltpu.VMEM((frames, heads_width), BF16),
            pltpu.VMEM((frames, heads_width), BF16),
            pltpu.VMEM((frames, 3 * frames), F32),
            pltpu.VMEM((HEADS, frames, 3 * frames), F32),
            pltpu.VMEM((frames, width), F32),
            pltpu.VMEM((micro, frames + 16, width), F32),
            pltpu.VMEM((micro, frames, width), BF16),
            dma((2,)),
            dma((3,)),
            dma((3,)),
            dma((4, 2, steps)),
            dma((4, 2, steps)),
            dma((4, 2 * steps)),
            dma((4, 2 * steps)),
            dma((2 * steps,)),
            dma((2 * steps,)),
            dma((micro, 4, 2)),
            dma((micro, 4, 2)),
            dma((micro, 2)),
            dma((micro, 2)),
            dma((micro, 4)),
            dma((micro, 4)),
            dma((micro,)),
        ],
        compiler_params=pltpu.CompilerParams(
            collective_id=0, has_side_effects=True, vmem_limit_bytes=48 * 1024 * 1024
        ),
    )(lengths, grouped, stem_weight, w_qkv[0], w_out[0], norm_gains[0], conv_kernel[0])
    return arrived[None]


def solution(mesh):
    return jax.shard_map(
        functools.partial(shards, mesh.shape["section"], mesh.shape["seq"]),
        mesh=mesh,
        in_specs=(
            P("dp", "seq", None),
            P("dp"),
            P(("seq", "dp"), None),
            P("section", ("seq", "dp"), None),
            P("section", ("seq", "dp"), None),
            P("section", None, None),
            P("section", None, None),
        ),
        out_specs=P("section", "dp", "seq", None),
        check_vma=False,
    )
```

```python
import functools

import jax
import jax.numpy as jnp
from jax import lax
from jax.experimental import pallas as pl
from jax.experimental.pallas import tpu as pltpu
from jax.sharding import PartitionSpec as P

HEADS = 8
STRIDE = 4
UNITS = ((16, 16), (32, 16), (48, 32), (80, 32), (0, 16), (112, 16))
DETOURS = 2
RIM_UNIT = 4
GROUPS = ((2,), (3, 0), (1, 4, 5))
eps = 1e-05
masked_score = -1e30
F32 = jnp.float32
BF16 = jnp.bfloat16
MESH = pl.DeviceIdType.MESH


def remote(src, dst, send, recv, **device):
    return pltpu.make_async_remote_copy(
        src_ref=src, dst_ref=dst, send_sem=send, recv_sem=recv, device_id=device, device_id_type=MESH
    )


def rows(ref, start, count):
    return ref.at[pl.ds(pl.multiple_of(start, 16), count)]


def kernel(
    sections, nseq,
    lengths, grouped, stem_in, qkv_in, out_in, gains, taps, arrivals,
    stem_full, qkv_full, out_full, out_peer, xs, normed, kv, queries, context, mask, scores, stream, conv_in, result, passing,
    local_sem, pair_send, pair_recv, ring_send, ring_recv, cross_send, cross_recv, pass_send, pass_recv,
    halo_send, halo_recv, rim_send, rim_recv, relay_send, relay_recv, passing_send, passing_recv, done_sem,
):
    section = lax.axis_index("section")
    seq = lax.axis_index("seq")
    dp = lax.axis_index("dp")
    nz = nseq // 2
    z, core = lax.div(seq, 2), lax.rem(seq, 2)
    ahead = lax.rem(z + 1, nz) * 2 + core
    behind = lax.rem(z + nz - 1, nz) * 2 + core
    other = seq + 1 - 2 * core
    right, left = lax.rem(seq + 1, nseq), lax.rem(seq + nseq - 1, nseq)
    far = jnp.where(core == 1, right, left)
    following, preceding = lax.rem(section + 1, sections), lax.rem(section + sections - 1, sections)
    partner = lax.rem(section + sections // 2, sections)
    beside_following, beside_source = lax.rem(partner + 1, sections), lax.rem(partner + sections - 1, sections)
    first = section == 0

    micro, frames, width = xs.shape[0] // 2, xs.shape[1], xs.shape[2]
    heads_width = queries.shape[1]
    head_size = heads_width // HEADS
    stem_rows, qkv_rows, out_rows = stem_in.shape[0], qkv_in.shape[0], out_in.shape[0]

    barrier = pltpu.get_barrier_semaphore()
    for device in (
        {"seq": ahead}, {"seq": behind}, {"seq": other}, {"seq": far},
        {"dp": 1 - dp}, {"section": following}, {"section": preceding},
        {"section": partner}, {"section": beside_following}, {"section": beside_source},
    ):
        pl.semaphore_signal(barrier, inc=1, device_id=device, device_id_type=MESH)
    pl.semaphore_wait(barrier, 10)

    def own_rows(full, count):
        return rows(full, (seq * 2 + dp) * count, count)

    stem_pair = remote(stem_in, own_rows(stem_full, stem_rows), pair_send.at[2], pair_recv.at[2], dp=1 - dp)
    stem_keep = pltpu.make_async_copy(stem_in, own_rows(stem_full, stem_rows), local_sem.at[1])
    qkv_pair = remote(qkv_in, own_rows(qkv_full, qkv_rows), pair_send.at[0], pair_recv.at[0], dp=1 - dp)
    qkv_keep = pltpu.make_async_copy(qkv_in, own_rows(qkv_full, qkv_rows), local_sem.at[0])
    out_pair = remote(out_in, out_peer, pair_send.at[1], pair_recv.at[1], dp=1 - dp)

    @pl.when(first)
    def _():
        stem_pair.start()
        stem_keep.start()

    qkv_pair.start()
    qkv_keep.start()
    out_pair.start()

    steps = nz // 2

    places = [
        [(lax.rem(z + nz - t, nz) * 2 + core) for t in range(steps + 1)],
        [(lax.rem(z + t, nz) * 2 + core) for t in range(steps)],
    ]
    out_cut = out_rows // 16 * 16
    arrays = {
        "stem": (0, stem_full, stem_rows, 0, 2 * stem_rows, stem_rows),
        "own": (1, qkv_full, qkv_rows, dp * qkv_rows, qkv_rows, qkv_rows),
        "peer": (2, qkv_full, qkv_rows, (1 - dp) * qkv_rows, qkv_rows, qkv_rows),
        "out": (3, out_full, out_rows, 0, 2 * out_rows, out_cut),
    }
    hops, crosses, pairs = {}, {}, {}
    for name, (index, full, count, low, size, cut) in arrays.items():
        for side in range(2):
            for t in range(0 if name == "peer" else steps):
                start, length = places[side][t] * (2 * count) + low, size
                if t == steps - 1:
                    start, length = (start, cut) if side == 0 else (start + cut, size - cut)
                if length:
                    src = rows(full, start, length)
                    hops[name, side, t] = remote(
                        src, src, ring_send.at[index, side, t], ring_recv.at[index, side, t],
                        seq=ahead if side == 0 else behind,
                    )
        for slot in range(2 * steps):
            place = places[0][slot] if slot <= steps else places[1][slot - steps]
            src = rows(full, place * (2 * count) + low, size)
            crosses[name, slot] = remote(src, src, cross_send.at[index, slot], cross_recv.at[index, slot], seq=other)
            if name == "own" and slot not in (0,):
                pairs[slot] = remote(src, src, pass_send.at[slot], pass_recv.at[slot], dp=1 - dp)

    def hop(name, side, t):
        return hops.get((name, side, t))

    def cross(name, slot):
        return crosses[name, slot]

    def ring_open(name):
        for side in range(2):
            if hop(name, side, 0) is not None:
                hop(name, side, 0).start()
        cross(name, 0).start()

    def ring_step(name, t):
        for side in range(2):
            slot = t if side == 0 else steps + t
            hop(name, side, t - 1).wait_recv()
            move = hop(name, side, t)
            if move is not None:
                move.start()
            cross(name, slot).start()
            if name == "own" and slot in pairs:
                pairs[slot].start()

    def ring_close(name):
        for side in range(2):
            move = hop(name, side, steps - 1)
            if move is not None:
                move.wait_recv()
        if name == "own":
            pairs[steps].start()
        if name != "peer":
            cross(name, steps).start()
        for slot in range(2 * steps):
            if name == "peer" and slot in pairs:
                pairs[slot].wait_recv()
                cross(name, slot).start()
        for slot in range(2 * steps):
            cross(name, slot).wait_recv()

    def ring_sent(name):
        for t in range(steps):
            for side in range(2):
                move = hop(name, side, t)
                if move is not None:
                    move.wait_send()
        for slot in range(2 * steps):
            cross(name, slot).wait_send()
            if name == "own" and slot in pairs:
                pairs[slot].wait_send()

    def positions(shape, dim):
        return lax.broadcasted_iota(jnp.int32, shape, dim)

    def valid_rows(m, start, count):
        return jnp.where(positions((count, 1), 0) < lengths[m] - seq * frames - start, 1.0, 0.0)

    def stem():
        for m in range(micro):
            for start in range(0, width, 256):
                value = jnp.dot(grouped[m], stem_full[:, start : start + 256], preferred_element_type=F32)
                value = value * jax.nn.sigmoid(value) * valid_rows(m, 0, frames)
                xs[micro + m, :, start : start + 256] = value.astype(BF16)

    qkv_keep.wait()
    ring_open("own")

    @pl.when(first)
    def _():
        stem_keep.wait()
        stem_pair.wait()
        ring_open("stem")

    qkv_pair.wait()
    ring_open("peer")
    out_pair.wait()
    mine, theirs = out_in[...], out_peer[...]
    both = jnp.concatenate(
        [jnp.where(dp == 0, mine, theirs), jnp.where(dp == 0, theirs, mine)], axis=0
    )
    out_full[pl.ds(pl.multiple_of(seq * 2 * out_rows, 16), 2 * out_rows)] = both

    @pl.when(first)
    def _():
        ring_step("stem", 1)

    ring_step("own", 1)
    ring_open("out")

    @pl.when(first)
    def _():
        ring_step("stem", 2)

    ring_step("own", 2)
    ring_step("out", 1)

    @pl.when(first)
    def _():
        ring_step("stem", 3)

    ring_step("own", 3)
    ring_step("out", 2)

    @pl.when(first)
    def _():
        ring_close("stem")
        stem()
        ring_sent("stem")

    ring_close("own")
    ring_close("peer")
    ring_step("out", 3)

    units = UNITS
    groups = GROUPS

    def relay(m, unit):
        start, count = units[unit]
        src = result.at[m, pl.ds(start, count)]
        if unit < DETOURS:
            dst = passing.at[m, pl.ds(start - units[0][0], count)]
            return remote(src, dst, relay_send.at[m, unit], passing_recv.at[m, unit], section=beside_following)
        dst = xs.at[m, pl.ds(start, count)]
        return remote(src, dst, relay_send.at[m, unit], relay_recv.at[m, unit], section=following)

    def onward(m, unit):
        start, count = units[unit]
        src = passing.at[m, pl.ds(start - units[0][0], count)]
        dst = xs.at[m, pl.ds(start, count)]
        return remote(src, dst, passing_send.at[m, unit], relay_recv.at[m, unit], section=partner)

    def arrive(m, unit):
        (onward if unit < DETOURS else relay)(m, unit).wait_recv()

    def pass_on():
        def one(m, carry):
            for unit in range(DETOURS):
                relay(m, unit).wait_recv()
                onward(m, unit).start()
            return carry

        lax.fori_loop(0, micro, one, 0)

    def halo(m, unit, side):
        start, count = units[unit]
        src = kv.at[m, pl.ds(frames + start, count)]
        dst = kv.at[m, pl.ds(2 * frames * side + start, count)]
        return remote(
            src, dst, halo_send.at[m, unit, side], halo_recv.at[m, unit, side], seq=right if side == 0 else left
        )

    near_side, far_side = 1 - core, core
    near_keys = pl.multiple_of(frames * (1 - core), 128)
    far_keys = pl.multiple_of(2 * frames * core, 128)

    def halo_wait(m, side):
        for unit, (start, count) in enumerate(units):
            src = kv.at[m, pl.ds(frames + start, count)]
            dst = rows(kv.at[m], 2 * frames * side + start, count)
            remote(src, dst, halo_send.at[m, unit, side], halo_recv.at[m, unit, side], seq=right).wait_recv()

    def rim(m, side):
        src = conv_in.at[m, pl.ds(frames if side == 0 else 8, 8)]
        dst = conv_in.at[m, pl.ds(0 if side == 0 else 8 + frames, 8)]
        return remote(src, dst, rim_send.at[m, side], rim_recv.at[m, side], seq=right if side == 0 else left)

    def keep(m):
        return pltpu.make_async_copy(xs.at[m], arrivals.at[m], done_sem.at[m])

    def norm(value, gain):
        average = jnp.mean(value, axis=-1, keepdims=True)
        centered = value - average
        variance = jnp.mean(centered * centered, axis=-1, keepdims=True)
        return centered * lax.rsqrt(variance + eps) * gain

    def layer(m, carry):
        length = lengths[m]
        span = 3 * frames
        query = positions((frames, span), 0)
        column = positions((frames, span), 1)
        key = jnp.where(column < 2 * frames, column + near_keys, column + (far_keys - 2 * frames))
        place = seq * frames - frames + key
        allowed = (place >= 0) & (place < length) & (key >= query) & (key <= query + 2 * frames)
        mask[...] = jnp.where(allowed, 0.0, masked_score).astype(F32)

        slot = jnp.where(first, micro + m, m)
        for group in groups:
            @pl.when(jnp.logical_not(first))
            def _():
                for unit in group:
                    arrive(m, unit)

            for unit in group:
                for start in range(units[unit][0], sum(units[unit]), 16):
                    value = xs[slot, start : start + 16, :].astype(F32)
                    normed[start : start + 16, :] = norm(value, gains[0:1, :]).astype(BF16)
            some = [normed[units[unit][0] : sum(units[unit]), :] for unit in group]
            some = some[0] if len(some) == 1 else jnp.concatenate(some, axis=0)
            for start in range(0, 2 * heads_width, 256):
                at = heads_width + start
                value = jnp.dot(some, qkv_full[:, at : at + 256], preferred_element_type=F32).astype(BF16)
                low = 0
                for unit in group:
                    at, count = units[unit]
                    kv[m, frames + at : frames + at + count, start : start + 256] = value[low : low + count]
                    low += count
            for unit in group:
                for side in range(2):
                    halo(m, unit, side).start()

        @pl.when(jnp.logical_not(first))
        def _():
            keep(m).start()

        for start in range(0, heads_width, 256):
            value = jnp.dot(normed[...], qkv_full[:, start : start + 256], preferred_element_type=F32)
            queries[:, start : start + 256] = value.astype(BF16)
        windows = []
        for h in range(HEADS):
            base, low = h // 4 * 4 * head_size, h % 4 * head_size
            windows.append((base, low, low + head_size, low // 128 * 128, -(-(low + head_size) // 128) * 128))

        def score(first_key, count, at):
            for h, (base, low, high, lane_low, lane_high) in enumerate(windows):
                lane = positions((frames, lane_high - lane_low), 1) + lane_low
                q = queries[:, base + lane_low : base + lane_high]
                q = jnp.where((lane >= low) & (lane < high), q, jnp.zeros_like(q))
                k = kv[m, pl.ds(first_key, count), base + lane_low : base + lane_high]
                scores[h, :, at : at + count] = lax.dot_general(
                    q, k, (((1,), (1,)), ((), ())), preferred_element_type=F32
                )

        halo_wait(m, near_side)
        score(near_keys, 2 * frames, 0)
        halo_wait(m, far_side)
        score(far_keys, frames, 2 * frames)

        scale = 1.0 / head_size**0.5
        lane = positions((frames, 128), 1)
        for group in range(HEADS // 4):
            outs = []
            for h in range(4 * group, 4 * group + 4):
                base, low, high, lane_low, lane_high = windows[h]
                columns = slice(heads_width + base + lane_low, heads_width + base + lane_high)
                value = scores[h] * scale + mask[...]
                expon = jnp.exp(value - jnp.max(value, axis=-1, keepdims=True))
                total = jnp.sum(expon, axis=-1, keepdims=True)
                probs = expon.astype(BF16)
                value = jnp.dot(
                    probs[:, : 2 * frames], kv[m, pl.ds(near_keys, 2 * frames), columns], preferred_element_type=F32
                ) + jnp.dot(
                    probs[:, 2 * frames :], kv[m, pl.ds(far_keys, frames), columns], preferred_element_type=F32
                )
                outs.append(value * (1.0 / total))
            tiles = [
                jnp.where(lane < 96, outs[0], outs[1][:, :128]),
                jnp.where(lane < 64, outs[1][:, 128:], outs[2][:, :128]),
                jnp.where(lane < 32, outs[2][:, 128:], outs[3]),
            ]
            for index, tile in enumerate(tiles):
                at = 4 * head_size * group + index * 128
                context[:, at : at + 128] = tile.astype(BF16)

        @pl.when(m == 0)
        def _():
            ring_close("out")

        for start in range(0, width, 256):
            value = jnp.dot(context[...], out_full[:, start : start + 256], preferred_element_type=F32)
            stream[:, start : start + 256] = value + xs[slot, :, start : start + 256].astype(F32)

        for start in range(0, frames, 16):
            value = norm(stream[start : start + 16, :], gains[1:2, :]) * valid_rows(m, start, 16)
            conv_in[m, 8 + start : 8 + start + 16, :] = value.astype(BF16).astype(F32)
        for side in range(2):
            rim(m, side).start()
        count = taps.shape[0]
        for unit in range(len(units)):
            if unit == RIM_UNIT:
                for side in range(2):
                    rim(m, side).wait_recv()
                top, bottom = conv_in[m, 0:8, :], conv_in[m, 8 + frames : 16 + frames, :]
                conv_in[m, 0:8, :] = jnp.where(seq == 0, 0.0, top)
                conv_in[m, 8 + frames : 16 + frames, :] = jnp.where(seq == nseq - 1, 0.0, bottom)
            for start in range(units[unit][0], sum(units[unit]), 16):
                conv = jnp.zeros((16, width), F32)
                for offset in range(count):
                    at = 8 - count // 2 + start + offset
                    conv = conv + conv_in[m, at : at + 16, :] * taps[offset : offset + 1, :]
                value = (stream[start : start + 16, :] + conv * jax.nn.sigmoid(conv)) * valid_rows(m, start, 16)
                result[m, start : start + 16, :] = value.astype(BF16)
            relay(m, unit).start()
        return carry

    @pl.when(section > sections // 2)
    def _():
        pass_on()

    lax.fori_loop(0, micro, layer, 0)

    @pl.when(section <= sections // 2)
    def _():
        pass_on()

    @pl.when(first)
    def _():
        for m in range(micro):
            for unit in range(len(units)):
                arrive(m, unit)
            keep(m).start()

    for name in ("own", "peer", "out"):
        ring_sent(name)
    for m in range(micro):
        for unit in range(len(units)):
            relay(m, unit).wait_send()
            if unit < DETOURS:
                onward(m, unit).wait_send()
            for side in range(2):
                halo(m, unit, side).wait_send()
        for side in range(2):
            rim(m, side).wait_send()
        keep(m).wait()


def shards(sections, nseq, mel, lengths, stem_weight, w_qkv, w_out, norm_gains, conv_kernel):
    micro = mel.shape[0]
    frames = mel.shape[1] // STRIDE
    width = stem_weight.shape[1]
    heads_width = w_qkv.shape[2] // 3
    grouped = mel.reshape(micro, frames, STRIDE * mel.shape[2])
    depth, full_out = w_qkv.shape[1] * 2 * nseq, w_out.shape[1] * 2 * nseq
    steps = nseq // 4
    dma = pltpu.SemaphoreType.DMA
    vmem = pl.BlockSpec(memory_space=pltpu.VMEM)
    arrived = pl.pallas_call(
        functools.partial(kernel, sections, nseq),
        out_shape=jax.ShapeDtypeStruct((micro, frames, width), BF16),
        in_specs=[pl.BlockSpec(memory_space=pltpu.SMEM)] + [vmem] * 6,
        out_specs=pl.BlockSpec(memory_space=pl.ANY),
        scratch_shapes=[
            pltpu.VMEM((stem_weight.shape[0] * 2 * nseq, width), BF16),
            pltpu.VMEM((depth, 3 * heads_width), BF16),
            pltpu.VMEM((full_out, width), BF16),
            pltpu.VMEM(w_out.shape[1:], BF16),
            pltpu.VMEM((2 * micro, frames, width), BF16),
            pltpu.VMEM((frames, width), BF16),
            pltpu.VMEM((micro, 3 * frames, 2 * heads_width), BF16),
            pltpu.VMEM((frames, heads_width), BF16),
            pltpu.VMEM((frames, heads_width), BF16),
            pltpu.VMEM((frames, 3 * frames), F32),
            pltpu.VMEM((HEADS, frames, 3 * frames), F32),
            pltpu.VMEM((frames, width), F32),
            pltpu.VMEM((micro, frames + 16, width), F32),
            pltpu.VMEM((micro, frames, width), BF16),
            pltpu.VMEM((micro, sum(count for _, count in UNITS[:DETOURS]), width), BF16),
            dma((2,)),
            dma((3,)),
            dma((3,)),
            dma((4, 2, steps)),
            dma((4, 2, steps)),
            dma((4, 2 * steps)),
            dma((4, 2 * steps)),
            dma((2 * steps,)),
            dma((2 * steps,)),
            dma((micro, len(UNITS), 2)),
            dma((micro, len(UNITS), 2)),
            dma((micro, 2)),
            dma((micro, 2)),
            dma((micro, len(UNITS))),
            dma((micro, len(UNITS))),
            dma((micro, DETOURS)),
            dma((micro, DETOURS)),
            dma((micro,)),
        ],
        compiler_params=pltpu.CompilerParams(
            collective_id=0, has_side_effects=True, vmem_limit_bytes=48 * 1024 * 1024
        ),
    )(lengths, grouped, stem_weight, w_qkv[0], w_out[0], norm_gains[0], conv_kernel[0])
    return arrived[None]


def solution(mesh):
    return jax.shard_map(
        functools.partial(shards, mesh.shape["section"], mesh.shape["seq"]),
        mesh=mesh,
        in_specs=(
            P("dp", "seq", None),
            P("dp"),
            P(("seq", "dp"), None),
            P("section", ("seq", "dp"), None),
            P("section", ("seq", "dp"), None),
            P("section", None, None),
            P("section", None, None),
        ),
        out_specs=P("section", "dp", "seq", None),
        check_vma=False,
    )
```

```python
import functools

import jax
import jax.numpy as jnp
from jax import lax
from jax.experimental import pallas as pl
from jax.experimental.pallas import tpu as pltpu
from jax.sharding import PartitionSpec as P

HEADS = 8
STRIDE = 4
UNITS = ((16, 16), (32, 16), (48, 32), (80, 32), (0, 16), (112, 16))
DETOURS = 2
RIM_UNIT = 4
GROUPS = ((2,), (3, 0), (1, 4, 5))
PIECES = tuple(
    (unit, part, parts)
    for group in GROUPS
    for part, parts in (((0, 1), (1, 1)) if group == GROUPS[-1] else ((0, 2),))
    for unit in group
)
eps = 1e-05
masked_score = -1e30
F32 = jnp.float32
BF16 = jnp.bfloat16
MESH = pl.DeviceIdType.MESH


def remote(src, dst, send, recv, **device):
    return pltpu.make_async_remote_copy(
        src_ref=src, dst_ref=dst, send_sem=send, recv_sem=recv, device_id=device, device_id_type=MESH
    )


def rows(ref, start, count):
    return ref.at[pl.ds(pl.multiple_of(start, 16), count)]


def kernel(
    sections, nseq,
    lengths, mel, stem_in, qkv_in, out_in, gains, taps, arrivals,
    stem_full, qkv_full, out_full, out_peer, xs, normed, kv, queries, context, mask, scores, stream, conv_in, result, passing,
    mel_wide, local_sem, stem_send, stem_recv, pair_send, pair_recv, ring_send, ring_recv, cross_send, cross_recv, pass_send, pass_recv,
    halo_send, halo_recv, rim_send, rim_recv, relay_send, relay_recv, passing_send, passing_recv, done_sem,
):
    section = lax.axis_index("section")
    seq = lax.axis_index("seq")
    dp = lax.axis_index("dp")
    nz = nseq // 2
    z, core = lax.div(seq, 2), lax.rem(seq, 2)
    ahead = lax.rem(z + 1, nz) * 2 + core
    behind = lax.rem(z + nz - 1, nz) * 2 + core
    other = seq + 1 - 2 * core
    right, left = lax.rem(seq + 1, nseq), lax.rem(seq + nseq - 1, nseq)
    far = jnp.where(core == 1, right, left)
    following, preceding = lax.rem(section + 1, sections), lax.rem(section + sections - 1, sections)
    partner = lax.rem(section + sections // 2, sections)
    beside_following, beside_source = lax.rem(partner + 1, sections), lax.rem(partner + sections - 1, sections)
    first = section == 0
    makes_stem = section == sections // 2 - 1

    micro, frames, width = xs.shape[0] // 2, xs.shape[1], xs.shape[2]
    heads_width = queries.shape[1]
    head_size = heads_width // HEADS
    stem_rows, qkv_rows, out_rows = stem_in.shape[0], qkv_in.shape[0], out_in.shape[0]

    barrier = pltpu.get_barrier_semaphore()
    for device in (
        {"seq": ahead}, {"seq": behind}, {"seq": other}, {"seq": far},
        {"dp": 1 - dp}, {"section": following}, {"section": preceding},
        {"section": partner}, {"section": beside_following}, {"section": beside_source},
    ):
        pl.semaphore_signal(barrier, inc=1, device_id=device, device_id_type=MESH)
    pl.semaphore_wait(barrier, 10)

    def own_rows(full, count):
        return rows(full, (seq * 2 + dp) * count, count)

    stem_pair = remote(stem_in, own_rows(stem_full, stem_rows), pair_send.at[2], pair_recv.at[2], dp=1 - dp)
    stem_keep = pltpu.make_async_copy(stem_in, own_rows(stem_full, stem_rows), local_sem.at[1])
    qkv_pair = remote(qkv_in, own_rows(qkv_full, qkv_rows), pair_send.at[0], pair_recv.at[0], dp=1 - dp)
    qkv_keep = pltpu.make_async_copy(qkv_in, own_rows(qkv_full, qkv_rows), local_sem.at[0])
    out_pair = remote(out_in, out_peer, pair_send.at[1], pair_recv.at[1], dp=1 - dp)

    @pl.when(makes_stem)
    def _():
        stem_pair.start()
        stem_keep.start()

    qkv_pair.start()
    qkv_keep.start()
    out_pair.start()

    steps = nz // 2

    places = [
        [(lax.rem(z + nz - t, nz) * 2 + core) for t in range(steps + 1)],
        [(lax.rem(z + t, nz) * 2 + core) for t in range(steps)],
    ]
    out_cut = out_rows // 16 * 16
    arrays = {
        "stem": (0, stem_full, stem_rows, 0, 2 * stem_rows, stem_rows),
        "own": (1, qkv_full, qkv_rows, dp * qkv_rows, qkv_rows, qkv_rows),
        "peer": (2, qkv_full, qkv_rows, (1 - dp) * qkv_rows, qkv_rows, qkv_rows),
        "out": (3, out_full, out_rows, 0, 2 * out_rows, out_cut),
    }
    hops, crosses, pairs = {}, {}, {}
    for name, (index, full, count, low, size, cut) in arrays.items():
        for side in range(2):
            for t in ((steps - 2,) if name == "peer" else range(steps)):
                start, length = places[side][t] * (2 * count) + low, size
                if t == steps - 1 and name != "peer":
                    start, length = (start, cut) if side == 0 else (start + cut, size - cut)
                if length:
                    src = rows(full, start, length)
                    hops[name, side, t] = remote(
                        src, src, ring_send.at[index, side, t], ring_recv.at[index, side, t],
                        seq=ahead if side == 0 else behind,
                    )
        for slot in range(2 * steps):
            place = places[0][slot] if slot <= steps else places[1][slot - steps]
            src = rows(full, place * (2 * count) + low, size)
            crosses[name, slot] = remote(src, src, cross_send.at[index, slot], cross_recv.at[index, slot], seq=other)
            if name == "own" and slot not in (0, steps - 1, 2 * steps - 1):
                pairs[slot] = remote(src, src, pass_send.at[slot], pass_recv.at[slot], dp=1 - dp)

    def hop(name, side, t):
        return hops.get((name, side, t))

    def cross(name, slot):
        return crosses[name, slot]

    def ring_open(name):
        for side in range(2):
            if hop(name, side, 0) is not None:
                hop(name, side, 0).start()
        cross(name, 0).start()

    def ring_step(name, t):
        for side in range(2):
            slot = t if side == 0 else steps + t
            hop(name, side, t - 1).wait_recv()
            move = hop(name, side, t)
            if move is not None:
                move.start()
            cross(name, slot).start()
            if name == "own" and slot in pairs:
                pairs[slot].start()

    def ring_close(name):
        for side in range(2):
            move = hop(name, side, steps - 1)
            if move is not None:
                move.wait_recv()
        if name == "own":
            pairs[steps].start()
        if name != "peer":
            cross(name, steps).start()
        if name == "peer":
            for slot in [t + side * steps for t in range(1, steps - 1) for side in range(2)] + [steps]:
                pairs[slot].wait_recv()
                cross(name, slot).start()
                if slot in (steps - 2, 2 * steps - 2):
                    hop(name, slot // steps, steps - 2).start()
            for side in range(2):
                hop(name, side, steps - 2).wait_recv()
                cross(name, steps - 1 + side * steps).start()
        for slot in range(2 * steps):
            cross(name, slot).wait_recv()

    def ring_sent(name):
        for t in range(steps):
            for side in range(2):
                move = hop(name, side, t)
                if move is not None:
                    move.wait_send()
        for slot in range(2 * steps):
            cross(name, slot).wait_send()
            if name == "own" and slot in pairs:
                pairs[slot].wait_send()

    def positions(shape, dim):
        return lax.broadcasted_iota(jnp.int32, shape, dim)

    def valid_rows(m, start, count):
        return jnp.where(positions((count, 1), 0) < lengths[m] - seq * frames - start, 1.0, 0.0)

    def stem_copy(m):
        whole = xs.at[micro + m]
        return remote(whole, whole, stem_send.at[m], stem_recv.at[m], section=beside_following)

    @pl.when(makes_stem)
    def _():
        stem_keep.wait()
        stem_pair.wait()
        ring_open("stem")
        for t in range(1, steps):
            ring_step("stem", t)
        ring_close("stem")
        for m in range(micro):
            mel_wide[...] = mel[m].astype(F32)
            joined = jnp.concatenate(
                [mel_wide[pl.ds(step, frames, stride=STRIDE), :].astype(BF16) for step in range(STRIDE)], axis=1
            )
            for start in range(0, width, 256):
                value = jnp.dot(joined, stem_full[:, start : start + 256], preferred_element_type=F32)
                value = value * jax.nn.sigmoid(value) * valid_rows(m, 0, frames)
                xs[micro + m, :, start : start + 256] = value.astype(BF16)
            stem_copy(m).start()
        ring_sent("stem")

    qkv_keep.wait()
    ring_open("own")

    qkv_pair.wait()
    ring_open("peer")
    out_pair.wait()
    mine, theirs = out_in[...], out_peer[...]
    both = jnp.concatenate(
        [jnp.where(dp == 0, mine, theirs), jnp.where(dp == 0, theirs, mine)], axis=0
    )
    out_full[pl.ds(pl.multiple_of(seq * 2 * out_rows, 16), 2 * out_rows)] = both

    ring_step("own", 1)
    ring_open("out")

    ring_step("own", 2)
    ring_step("out", 1)

    ring_step("own", 3)
    ring_step("out", 2)

    ring_close("own")
    ring_close("peer")
    ring_step("out", 3)

    @pl.when(jnp.logical_not(first))
    def _():
        ring_close("out")


    units = UNITS
    groups = GROUPS

    def relay(m, unit):
        start, count = units[unit]
        src = result.at[m, pl.ds(start, count)]
        if unit < DETOURS:
            dst = passing.at[m, pl.ds(start - units[0][0], count)]
            return remote(src, dst, relay_send.at[m, unit], passing_recv.at[m, unit], section=beside_following)
        dst = xs.at[m, pl.ds(start, count)]
        return remote(src, dst, relay_send.at[m, unit], relay_recv.at[m, unit], section=following)

    def onward(m, unit):
        start, count = units[unit]
        src = passing.at[m, pl.ds(start - units[0][0], count)]
        dst = xs.at[m, pl.ds(start, count)]
        return remote(src, dst, passing_send.at[m, unit], relay_recv.at[m, unit], section=partner)

    def arrive(m, unit):
        (onward if unit < DETOURS else relay)(m, unit).wait_recv()

    def pass_on():
        def one(m, carry):
            for unit in range(DETOURS):
                relay(m, unit).wait_recv()
                onward(m, unit).start()
            return carry

        lax.fori_loop(0, micro, one, 0)

    def halo(m, index, side):
        unit, part, parts = PIECES[index]
        start, count = units[unit]
        columns = pl.ds(part * heads_width, parts * heads_width)
        src = kv.at[m, pl.ds(frames + start, count), columns]
        dst = kv.at[m, pl.ds(2 * frames * side + start, count), columns]
        return remote(
            src, dst, halo_send.at[m, index, side], halo_recv.at[m, index, side], seq=right if side == 0 else left
        )

    near_side, far_side = 1 - core, core
    near_keys = pl.multiple_of(frames * (1 - core), 128)
    far_keys = pl.multiple_of(2 * frames * core, 128)

    def halo_wait(m, side, wanted):
        for index, (unit, part, parts) in enumerate(PIECES):
            if part == wanted:
                start, count = units[unit]
                columns = pl.ds(part * heads_width, parts * heads_width)
                src = kv.at[m, pl.ds(frames + start, count), columns]
                dst = kv.at[m, pl.ds(pl.multiple_of(2 * frames * side + start, 16), count), columns]
                remote(src, dst, halo_send.at[m, index, side], halo_recv.at[m, index, side], seq=right).wait_recv()

    def rim(m, side):
        src = conv_in.at[m, pl.ds(frames if side == 0 else 8, 8)]
        dst = conv_in.at[m, pl.ds(0 if side == 0 else 8 + frames, 8)]
        return remote(src, dst, rim_send.at[m, side], rim_recv.at[m, side], seq=right if side == 0 else left)

    def keep(m):
        return pltpu.make_async_copy(xs.at[m], arrivals.at[m], done_sem.at[m])

    def norm(value, gain):
        average = jnp.mean(value, axis=-1, keepdims=True)
        centered = value - average
        variance = jnp.mean(centered * centered, axis=-1, keepdims=True)
        return centered * lax.rsqrt(variance + eps) * gain

    def layer(m, carry):
        length = lengths[m]
        span = 3 * frames
        query = positions((frames, span), 0)
        column = positions((frames, span), 1)
        key = jnp.where(column < 2 * frames, column + near_keys, column + (far_keys - 2 * frames))
        place = seq * frames - frames + key
        allowed = (place >= 0) & (place < length) & (key >= query) & (key <= query + 2 * frames)
        mask[...] = jnp.where(allowed, 0.0, masked_score).astype(F32)

        slot = jnp.where(first, micro + m, m)

        @pl.when(first)
        def _():
            stem_copy(m).wait_recv()

        for group in groups:
            @pl.when(jnp.logical_not(first))
            def _():
                for unit in group:
                    arrive(m, unit)

            for unit in group:
                for start in range(units[unit][0], sum(units[unit]), 16):
                    value = xs[slot, start : start + 16, :].astype(F32)
                    normed[start : start + 16, :] = norm(value, gains[0:1, :]).astype(BF16)
            some = [normed[units[unit][0] : sum(units[unit]), :] for unit in group]
            some = some[0] if len(some) == 1 else jnp.concatenate(some, axis=0)
            for part in range(2):
                for start in range(part * heads_width, (part + 1) * heads_width, 256):
                    at = heads_width + start
                    value = jnp.dot(some, qkv_full[:, at : at + 256], preferred_element_type=F32).astype(BF16)
                    low = 0
                    for unit in group:
                        at, count = units[unit]
                        kv[m, frames + at : frames + at + count, start : start + 256] = value[low : low + count]
                        low += count
                for index, (unit, first_part, parts) in enumerate(PIECES):
                    if unit in group and first_part + parts - 1 == part:
                        for side in range(2):
                            halo(m, index, side).start()

        @pl.when(jnp.logical_not(first))
        def _():
            keep(m).start()

        for start in range(0, heads_width, 256):
            value = jnp.dot(normed[...], qkv_full[:, start : start + 256], preferred_element_type=F32)
            queries[:, start : start + 256] = value.astype(BF16)
        windows = []
        for h in range(HEADS):
            base, low = h // 4 * 4 * head_size, h % 4 * head_size
            windows.append((base, low, low + head_size, low // 128 * 128, -(-(low + head_size) // 128) * 128))

        def score(first_key, count, at):
            for h, (base, low, high, lane_low, lane_high) in enumerate(windows):
                lane = positions((frames, lane_high - lane_low), 1) + lane_low
                q = queries[:, base + lane_low : base + lane_high]
                q = jnp.where((lane >= low) & (lane < high), q, jnp.zeros_like(q))
                k = kv[m, pl.ds(first_key, count), base + lane_low : base + lane_high]
                scores[h, :, at : at + count] = lax.dot_general(
                    q, k, (((1,), (1,)), ((), ())), preferred_element_type=F32
                )

        halo_wait(m, near_side, 0)
        score(near_keys, 2 * frames, 0)
        halo_wait(m, far_side, 0)
        score(far_keys, frames, 2 * frames)
        halo_wait(m, near_side, 1)
        halo_wait(m, far_side, 1)

        scale = 1.0 / head_size**0.5
        lane = positions((frames, 128), 1)
        for group in range(HEADS // 4):
            outs = []
            for h in range(4 * group, 4 * group + 4):
                base, low, high, lane_low, lane_high = windows[h]
                columns = slice(heads_width + base + lane_low, heads_width + base + lane_high)
                value = scores[h] * scale + mask[...]
                expon = jnp.exp(value - jnp.max(value, axis=-1, keepdims=True))
                total = jnp.sum(expon, axis=-1, keepdims=True)
                probs = expon.astype(BF16)
                value = jnp.dot(
                    probs[:, : 2 * frames], kv[m, pl.ds(near_keys, 2 * frames), columns], preferred_element_type=F32
                ) + jnp.dot(
                    probs[:, 2 * frames :], kv[m, pl.ds(far_keys, frames), columns], preferred_element_type=F32
                )
                outs.append(value * (1.0 / total))
            tiles = [
                jnp.where(lane < 96, outs[0], outs[1][:, :128]),
                jnp.where(lane < 64, outs[1][:, 128:], outs[2][:, :128]),
                jnp.where(lane < 32, outs[2][:, 128:], outs[3]),
            ]
            for index, tile in enumerate(tiles):
                at = 4 * head_size * group + index * 128
                context[:, at : at + 128] = tile.astype(BF16)

        @pl.when(first & (m == 0))
        def _():
            ring_close("out")

        for start in range(0, width, 256):
            value = jnp.dot(context[...], out_full[:, start : start + 256], preferred_element_type=F32)
            stream[:, start : start + 256] = value + xs[slot, :, start : start + 256].astype(F32)

        ready = set()

        def prepare(starts):
            for start in starts:
                if start in ready or not 0 <= start < frames:
                    continue
                ready.add(start)
                value = norm(stream[start : start + 16, :], gains[1:2, :]) * valid_rows(m, start, 16)
                conv_in[m, 8 + start : 8 + start + 16, :] = value.astype(BF16).astype(F32)

        prepare((0, frames - 16))
        for side in range(2):
            rim(m, side).start()

        count = taps.shape[0]
        for unit in range(len(units)):
            if unit == RIM_UNIT:
                for side in range(2):
                    rim(m, side).wait_recv()
                top, bottom = conv_in[m, 0:8, :], conv_in[m, 8 + frames : 16 + frames, :]
                conv_in[m, 0:8, :] = jnp.where(seq == 0, 0.0, top)
                conv_in[m, 8 + frames : 16 + frames, :] = jnp.where(seq == nseq - 1, 0.0, bottom)
            for start in range(units[unit][0], sum(units[unit]), 16):
                prepare((start - 16, start, start + 16))
                conv = jnp.zeros((16, width), F32)
                for offset in range(count):
                    at = 8 - count // 2 + start + offset
                    conv = conv + conv_in[m, at : at + 16, :] * taps[offset : offset + 1, :]
                value = (stream[start : start + 16, :] + conv * jax.nn.sigmoid(conv)) * valid_rows(m, start, 16)
                result[m, start : start + 16, :] = value.astype(BF16)
            relay(m, unit).start()
        return carry

    @pl.when(section > sections // 2)
    def _():
        pass_on()

    lax.fori_loop(0, micro, layer, 0)

    @pl.when(section <= sections // 2)
    def _():
        pass_on()

    @pl.when(first)
    def _():
        for m in range(micro):
            for unit in range(len(units)):
                arrive(m, unit)
            keep(m).start()

    @pl.when(makes_stem)
    def _():
        for m in range(micro):
            stem_copy(m).wait_send()

    for name in ("own", "peer", "out"):
        ring_sent(name)
    for m in range(micro):
        for unit in range(len(units)):
            relay(m, unit).wait_send()
            if unit < DETOURS:
                onward(m, unit).wait_send()
        for side in range(2):
            rim(m, side).wait_send()
            for index in range(len(PIECES)):
                halo(m, index, side).wait_send()
        keep(m).wait()


def shards(sections, nseq, mel, lengths, stem_weight, w_qkv, w_out, norm_gains, conv_kernel):
    micro = mel.shape[0]
    frames = mel.shape[1] // STRIDE
    width = stem_weight.shape[1]
    heads_width = w_qkv.shape[2] // 3
    depth, full_out = w_qkv.shape[1] * 2 * nseq, w_out.shape[1] * 2 * nseq
    steps = nseq // 4
    dma = pltpu.SemaphoreType.DMA
    vmem = pl.BlockSpec(memory_space=pltpu.VMEM)
    arrived = pl.pallas_call(
        functools.partial(kernel, sections, nseq),
        out_shape=jax.ShapeDtypeStruct((micro, frames, width), BF16),
        in_specs=[pl.BlockSpec(memory_space=pltpu.SMEM)] + [vmem] * 6,
        out_specs=pl.BlockSpec(memory_space=pl.ANY),
        scratch_shapes=[
            pltpu.VMEM((stem_weight.shape[0] * 2 * nseq, width), BF16),
            pltpu.VMEM((depth, 3 * heads_width), BF16),
            pltpu.VMEM((full_out, width), BF16),
            pltpu.VMEM(w_out.shape[1:], BF16),
            pltpu.VMEM((2 * micro, frames, width), BF16),
            pltpu.VMEM((frames, width), BF16),
            pltpu.VMEM((micro, 3 * frames, 2 * heads_width), BF16),
            pltpu.VMEM((frames, heads_width), BF16),
            pltpu.VMEM((frames, heads_width), BF16),
            pltpu.VMEM((frames, 3 * frames), F32),
            pltpu.VMEM((HEADS, frames, 3 * frames), F32),
            pltpu.VMEM((frames, width), F32),
            pltpu.VMEM((micro, frames + 16, width), F32),
            pltpu.VMEM((micro, frames, width), BF16),
            pltpu.VMEM((micro, sum(count for _, count in UNITS[:DETOURS]), width), BF16),
            pltpu.VMEM(mel.shape[1:], F32),
            dma((2,)),
            dma((micro,)),
            dma((micro,)),
            dma((3,)),
            dma((3,)),
            dma((4, 2, steps)),
            dma((4, 2, steps)),
            dma((4, 2 * steps)),
            dma((4, 2 * steps)),
            dma((2 * steps,)),
            dma((2 * steps,)),
            dma((micro, len(PIECES), 2)),
            dma((micro, len(PIECES), 2)),
            dma((micro, 2)),
            dma((micro, 2)),
            dma((micro, len(UNITS))),
            dma((micro, len(UNITS))),
            dma((micro, DETOURS)),
            dma((micro, DETOURS)),
            dma((micro,)),
        ],
        compiler_params=pltpu.CompilerParams(
            collective_id=0, has_side_effects=True, vmem_limit_bytes=48 * 1024 * 1024
        ),
    )(lengths, mel, stem_weight, w_qkv[0], w_out[0], norm_gains[0], conv_kernel[0])
    return arrived[None]


def solution(mesh):
    return jax.shard_map(
        functools.partial(shards, mesh.shape["section"], mesh.shape["seq"]),
        mesh=mesh,
        in_specs=(
            P("dp", "seq", None),
            P("dp"),
            P(("seq", "dp"), None),
            P("section", ("seq", "dp"), None),
            P("section", ("seq", "dp"), None),
            P("section", None, None),
            P("section", None, None),
        ),
        out_specs=P("section", "dp", "seq", None),
        check_vma=False,
    )
```

```python
import functools

import jax
import jax.numpy as jnp
from jax import lax
from jax.experimental import pallas as pl
from jax.experimental.pallas import tpu as pltpu
from jax.sharding import PartitionSpec as P

HEADS = 8
STRIDE = 4
UNITS = ((16, 16), (32, 16), (48, 32), (80, 32), (0, 16), (112, 16))
DETOURS = 2
RIM_UNIT = 4
GROUPS = ((2,), (3, 0), (1, 4, 5))
PIECES = tuple(
    (unit, part, parts)
    for group in GROUPS
    for part, parts in (((0, 1), (1, 1)) if group == GROUPS[-1] else ((0, 2),))
    for unit in group
)
eps = 1e-05
masked_score = -1e30
F32 = jnp.float32
BF16 = jnp.bfloat16
MESH = pl.DeviceIdType.MESH


def remote(src, dst, send, recv, **device):
    return pltpu.make_async_remote_copy(
        src_ref=src, dst_ref=dst, send_sem=send, recv_sem=recv, device_id=device, device_id_type=MESH
    )


def rows(ref, start, count):
    return ref.at[pl.ds(pl.multiple_of(start, 16), count)]


def kernel(
    sections, nseq,
    lengths, mel, stem_in, qkv_in, out_in, gains, taps, arrivals,
    stem_full, qkv_full, out_full, out_peer, xs, normed, kv, queries, context, mask, scores, stream, conv_in, result, passing,
    mel_wide, local_sem, stem_send, stem_recv, pair_send, pair_recv, ring_send, ring_recv, cross_send, cross_recv, pass_send, pass_recv,
    halo_send, halo_recv, rim_send, rim_recv, relay_send, relay_recv, passing_send, passing_recv, done_sem,
):
    section = lax.axis_index("section")
    seq = lax.axis_index("seq")
    dp = lax.axis_index("dp")
    nz = nseq // 2
    z, core = lax.div(seq, 2), lax.rem(seq, 2)
    ahead = lax.rem(z + 1, nz) * 2 + core
    behind = lax.rem(z + nz - 1, nz) * 2 + core
    other = seq + 1 - 2 * core
    right, left = lax.rem(seq + 1, nseq), lax.rem(seq + nseq - 1, nseq)
    far = jnp.where(core == 1, right, left)
    following, preceding = lax.rem(section + 1, sections), lax.rem(section + sections - 1, sections)
    partner = lax.rem(section + sections // 2, sections)
    beside_following, beside_source = lax.rem(partner + 1, sections), lax.rem(partner + sections - 1, sections)
    first = section == 0
    makes_stem = section == sections // 2 - 1

    micro, frames, width = xs.shape[0] // 2, xs.shape[1], xs.shape[2]
    heads_width = queries.shape[1]
    head_size = heads_width // HEADS
    stem_rows, qkv_rows, out_rows = stem_in.shape[0], qkv_in.shape[0], out_in.shape[0]

    barrier = pltpu.get_barrier_semaphore()
    for device in (
        {"seq": ahead}, {"seq": behind}, {"seq": other}, {"seq": far},
        {"dp": 1 - dp}, {"section": following}, {"section": preceding},
        {"section": partner}, {"section": beside_following}, {"section": beside_source},
    ):
        pl.semaphore_signal(barrier, inc=1, device_id=device, device_id_type=MESH)
    pl.semaphore_wait(barrier, 10)

    def own_rows(full, count):
        return rows(full, (seq * 2 + dp) * count, count)

    stem_pair = remote(stem_in, own_rows(stem_full, stem_rows), pair_send.at[2], pair_recv.at[2], dp=1 - dp)
    stem_keep = pltpu.make_async_copy(stem_in, own_rows(stem_full, stem_rows), local_sem.at[1])
    qkv_pair = remote(qkv_in, own_rows(qkv_full, qkv_rows), pair_send.at[0], pair_recv.at[0], dp=1 - dp)
    qkv_keep = pltpu.make_async_copy(qkv_in, own_rows(qkv_full, qkv_rows), local_sem.at[0])
    out_pair = remote(out_in, out_peer, pair_send.at[1], pair_recv.at[1], dp=1 - dp)

    @pl.when(makes_stem)
    def _():
        stem_pair.start()
        stem_keep.start()

    qkv_pair.start()
    qkv_keep.start()
    out_pair.start()

    steps = nz // 2

    places = [
        [(lax.rem(z + nz - t, nz) * 2 + core) for t in range(steps + 1)],
        [(lax.rem(z + t, nz) * 2 + core) for t in range(steps)],
    ]
    out_cut = out_rows // 16 * 16
    arrays = {
        "stem": (0, stem_full, stem_rows, 0, 2 * stem_rows, stem_rows),
        "own": (1, qkv_full, qkv_rows, dp * qkv_rows, qkv_rows, -(-qkv_rows // 32) * 16),
        "peer": (2, qkv_full, qkv_rows, (1 - dp) * qkv_rows, qkv_rows, qkv_rows),
        "out": (3, out_full, out_rows, 0, 2 * out_rows, out_cut),
    }
    hops, crosses, pairs = {}, {}, {}
    for name, (index, full, count, low, size, cut) in arrays.items():
        for side in range(2):
            for t in ((steps - 2,) if name == "peer" else range(steps)):
                start, length = places[side][t] * (2 * count) + low, size
                if t == steps - 1 and name != "peer":
                    start, length = (start, cut) if side == 0 else (start + cut, size - cut)
                if length:
                    src = rows(full, start, length)
                    hops[name, side, t] = remote(
                        src, src, ring_send.at[index, side, t], ring_recv.at[index, side, t],
                        seq=ahead if side == 0 else behind,
                    )
        for slot in range(2 * steps):
            place = places[0][slot] if slot <= steps else places[1][slot - steps]
            src = rows(full, place * (2 * count) + low, size)
            crosses[name, slot] = remote(src, src, cross_send.at[index, slot], cross_recv.at[index, slot], seq=other)
            if name == "own" and slot not in (0, steps - 1, 2 * steps - 1):
                pairs[slot] = remote(src, src, pass_send.at[slot], pass_recv.at[slot], dp=1 - dp)

    def hop(name, side, t):
        return hops.get((name, side, t))

    def cross(name, slot):
        return crosses[name, slot]

    def ring_open(name):
        for side in range(2):
            if hop(name, side, 0) is not None:
                hop(name, side, 0).start()
        cross(name, 0).start()

    def ring_step(name, t):
        for side in range(2):
            slot = t if side == 0 else steps + t
            hop(name, side, t - 1).wait_recv()
            move = hop(name, side, t)
            if move is not None:
                move.start()
            cross(name, slot).start()
            if name == "own" and slot in pairs:
                pairs[slot].start()

    def ring_close(name):
        for side in range(2):
            move = hop(name, side, steps - 1)
            if move is not None:
                move.wait_recv()
        if name == "own":
            pairs[steps].start()
        if name != "peer":
            cross(name, steps).start()
        if name == "peer":
            for slot in [t + side * steps for t in range(1, steps - 1) for side in range(2)] + [steps]:
                pairs[slot].wait_recv()
                cross(name, slot).start()
                if slot in (steps - 2, 2 * steps - 2):
                    hop(name, slot // steps, steps - 2).start()
            for side in range(2):
                hop(name, side, steps - 2).wait_recv()
                cross(name, steps - 1 + side * steps).start()
        for slot in range(2 * steps):
            cross(name, slot).wait_recv()

    def ring_sent(name):
        for t in range(steps):
            for side in range(2):
                move = hop(name, side, t)
                if move is not None:
                    move.wait_send()
        for slot in range(2 * steps):
            cross(name, slot).wait_send()
            if name == "own" and slot in pairs:
                pairs[slot].wait_send()

    def positions(shape, dim):
        return lax.broadcasted_iota(jnp.int32, shape, dim)

    def valid_rows(m, start, count):
        return jnp.where(positions((count, 1), 0) < lengths[m] - seq * frames - start, 1.0, 0.0)

    def stem_copy(m):
        whole = xs.at[micro + m]
        return remote(whole, whole, stem_send.at[m], stem_recv.at[m], section=beside_following)

    @pl.when(makes_stem)
    def _():
        stem_keep.wait()
        stem_pair.wait()
        ring_open("stem")
        for t in range(1, steps):
            ring_step("stem", t)
        ring_close("stem")
        for m in range(micro):
            mel_wide[...] = mel[m].astype(F32)
            joined = jnp.concatenate(
                [mel_wide[pl.ds(step, frames, stride=STRIDE), :].astype(BF16) for step in range(STRIDE)], axis=1
            )
            for start in range(0, width, 256):
                value = jnp.dot(joined, stem_full[:, start : start + 256], preferred_element_type=F32)
                value = value * jax.nn.sigmoid(value) * valid_rows(m, 0, frames)
                xs[micro + m, :, start : start + 256] = value.astype(BF16)
            stem_copy(m).start()
        ring_sent("stem")

    qkv_keep.wait()
    ring_open("own")

    qkv_pair.wait()
    ring_open("peer")
    out_pair.wait()
    mine, theirs = out_in[...], out_peer[...]
    both = jnp.concatenate(
        [jnp.where(dp == 0, mine, theirs), jnp.where(dp == 0, theirs, mine)], axis=0
    )
    out_full[pl.ds(pl.multiple_of(seq * 2 * out_rows, 16), 2 * out_rows)] = both

    ring_step("own", 1)
    ring_step("own", 2)
    ring_open("out")
    ring_step("own", 3)
    ring_step("out", 1)
    ring_close("own")
    ring_step("out", 2)
    ring_close("peer")
    ring_step("out", 3)

    @pl.when(jnp.logical_not(first))
    def _():
        ring_close("out")


    units = UNITS
    groups = GROUPS

    def relay(m, unit):
        start, count = units[unit]
        src = result.at[m, pl.ds(start, count)]
        if unit < DETOURS:
            dst = passing.at[m, pl.ds(start - units[0][0], count)]
            return remote(src, dst, relay_send.at[m, unit], passing_recv.at[m, unit], section=beside_following)
        dst = xs.at[m, pl.ds(start, count)]
        return remote(src, dst, relay_send.at[m, unit], relay_recv.at[m, unit], section=following)

    def onward(m, unit):
        start, count = units[unit]
        src = passing.at[m, pl.ds(start - units[0][0], count)]
        dst = xs.at[m, pl.ds(start, count)]
        return remote(src, dst, passing_send.at[m, unit], relay_recv.at[m, unit], section=partner)

    def arrive(m, unit):
        (onward if unit < DETOURS else relay)(m, unit).wait_recv()

    def pass_on():
        def one(m, carry):
            for unit in range(DETOURS):
                relay(m, unit).wait_recv()
                onward(m, unit).start()
            return carry

        lax.fori_loop(0, micro, one, 0)

    def halo(m, index, side):
        unit, part, parts = PIECES[index]
        start, count = units[unit]
        columns = pl.ds(part * heads_width, parts * heads_width)
        src = kv.at[m, pl.ds(frames + start, count), columns]
        dst = kv.at[m, pl.ds(2 * frames * side + start, count), columns]
        return remote(
            src, dst, halo_send.at[m, index, side], halo_recv.at[m, index, side], seq=right if side == 0 else left
        )

    near_side, far_side = 1 - core, core
    near_keys = pl.multiple_of(frames * (1 - core), 128)
    far_keys = pl.multiple_of(2 * frames * core, 128)

    def halo_wait(m, side, wanted):
        for index, (unit, part, parts) in enumerate(PIECES):
            if part == wanted:
                start, count = units[unit]
                columns = pl.ds(part * heads_width, parts * heads_width)
                src = kv.at[m, pl.ds(frames + start, count), columns]
                dst = kv.at[m, pl.ds(pl.multiple_of(2 * frames * side + start, 16), count), columns]
                remote(src, dst, halo_send.at[m, index, side], halo_recv.at[m, index, side], seq=right).wait_recv()

    def rim(m, side):
        src = conv_in.at[m, pl.ds(frames if side == 0 else 8, 8)]
        dst = conv_in.at[m, pl.ds(0 if side == 0 else 8 + frames, 8)]
        return remote(src, dst, rim_send.at[m, side], rim_recv.at[m, side], seq=right if side == 0 else left)

    def keep(m):
        return pltpu.make_async_copy(xs.at[m], arrivals.at[m], done_sem.at[m])

    def norm(value, gain):
        average = jnp.mean(value, axis=-1, keepdims=True)
        centered = value - average
        variance = jnp.mean(centered * centered, axis=-1, keepdims=True)
        return centered * lax.rsqrt(variance + eps) * gain

    def layer(m, carry):
        length = lengths[m]
        span = 3 * frames
        query = positions((frames, span), 0)
        column = positions((frames, span), 1)
        key = jnp.where(column < 2 * frames, column + near_keys, column + (far_keys - 2 * frames))
        place = seq * frames - frames + key
        allowed = (place >= 0) & (place < length) & (key >= query) & (key <= query + 2 * frames)
        mask[...] = jnp.where(allowed, 0.0, masked_score).astype(F32)

        slot = jnp.where(first, micro + m, m)

        @pl.when(first)
        def _():
            stem_copy(m).wait_recv()

        for group in groups:
            @pl.when(jnp.logical_not(first))
            def _():
                for unit in group:
                    arrive(m, unit)

            for unit in group:
                for start in range(units[unit][0], sum(units[unit]), 16):
                    value = xs[slot, start : start + 16, :].astype(F32)
                    normed[start : start + 16, :] = norm(value, gains[0:1, :]).astype(BF16)
            some = [normed[units[unit][0] : sum(units[unit]), :] for unit in group]
            some = some[0] if len(some) == 1 else jnp.concatenate(some, axis=0)
            for part in range(2):
                for start in range(part * heads_width, (part + 1) * heads_width, 256):
                    at = heads_width + start
                    value = jnp.dot(some, qkv_full[:, at : at + 256], preferred_element_type=F32).astype(BF16)
                    low = 0
                    for unit in group:
                        at, count = units[unit]
                        kv[m, frames + at : frames + at + count, start : start + 256] = value[low : low + count]
                        low += count
                for index, (unit, first_part, parts) in enumerate(PIECES):
                    if unit in group and first_part + parts - 1 == part:
                        for side in range(2):
                            halo(m, index, side).start()

        @pl.when(jnp.logical_not(first))
        def _():
            keep(m).start()

        for start in range(0, heads_width, 256):
            value = jnp.dot(normed[...], qkv_full[:, start : start + 256], preferred_element_type=F32)
            queries[:, start : start + 256] = value.astype(BF16)
        windows = []
        for h in range(HEADS):
            base, low = h // 4 * 4 * head_size, h % 4 * head_size
            windows.append((base, low, low + head_size, low // 128 * 128, -(-(low + head_size) // 128) * 128))

        def score(first_key, count, at):
            for h, (base, low, high, lane_low, lane_high) in enumerate(windows):
                lane = positions((frames, lane_high - lane_low), 1) + lane_low
                q = queries[:, base + lane_low : base + lane_high]
                q = jnp.where((lane >= low) & (lane < high), q, jnp.zeros_like(q))
                k = kv[m, pl.ds(first_key, count), base + lane_low : base + lane_high]
                scores[h, :, pl.ds(at, count)] = lax.dot_general(
                    q, k, (((1,), (1,)), ((), ())), preferred_element_type=F32
                )

        score(frames, frames, pl.multiple_of(frames * core, 128))
        halo_wait(m, near_side, 0)
        score(pl.multiple_of(2 * frames * (1 - core), 128), frames, pl.multiple_of(frames * (1 - core), 128))
        halo_wait(m, far_side, 0)
        score(far_keys, frames, 2 * frames)
        halo_wait(m, near_side, 1)
        halo_wait(m, far_side, 1)

        scale = 1.0 / head_size**0.5
        lane = positions((frames, 128), 1)
        for group in range(HEADS // 4):
            outs = []
            for h in range(4 * group, 4 * group + 4):
                base, low, high, lane_low, lane_high = windows[h]
                columns = slice(heads_width + base + lane_low, heads_width + base + lane_high)
                value = scores[h] * scale + mask[...]
                expon = jnp.exp(value - jnp.max(value, axis=-1, keepdims=True))
                total = jnp.sum(expon, axis=-1, keepdims=True)
                probs = expon.astype(BF16)
                value = jnp.dot(
                    probs[:, : 2 * frames], kv[m, pl.ds(near_keys, 2 * frames), columns], preferred_element_type=F32
                ) + jnp.dot(
                    probs[:, 2 * frames :], kv[m, pl.ds(far_keys, frames), columns], preferred_element_type=F32
                )
                outs.append(value * (1.0 / total))
            tiles = [
                jnp.where(lane < 96, outs[0], outs[1][:, :128]),
                jnp.where(lane < 64, outs[1][:, 128:], outs[2][:, :128]),
                jnp.where(lane < 32, outs[2][:, 128:], outs[3]),
            ]
            for index, tile in enumerate(tiles):
                at = 4 * head_size * group + index * 128
                context[:, at : at + 128] = tile.astype(BF16)

        @pl.when(first & (m == 0))
        def _():
            ring_close("out")

        for start in range(0, width, 256):
            value = jnp.dot(context[...], out_full[:, start : start + 256], preferred_element_type=F32)
            stream[:, start : start + 256] = value + xs[slot, :, start : start + 256].astype(F32)

        ready = set()

        def prepare(starts):
            for start in starts:
                if start in ready or not 0 <= start < frames:
                    continue
                ready.add(start)
                value = norm(stream[start : start + 16, :], gains[1:2, :]) * valid_rows(m, start, 16)
                conv_in[m, 8 + start : 8 + start + 16, :] = value.astype(BF16).astype(F32)

        prepare((0, frames - 16))
        for side in range(2):
            rim(m, side).start()

        count = taps.shape[0]
        for unit in range(len(units)):
            if unit == RIM_UNIT:
                for side in range(2):
                    rim(m, side).wait_recv()
                top, bottom = conv_in[m, 0:8, :], conv_in[m, 8 + frames : 16 + frames, :]
                conv_in[m, 0:8, :] = jnp.where(seq == 0, 0.0, top)
                conv_in[m, 8 + frames : 16 + frames, :] = jnp.where(seq == nseq - 1, 0.0, bottom)
            for start in range(units[unit][0], sum(units[unit]), 16):
                prepare((start - 16, start, start + 16))
                conv = jnp.zeros((16, width), F32)
                for offset in range(count):
                    at = 8 - count // 2 + start + offset
                    conv = conv + conv_in[m, at : at + 16, :] * taps[offset : offset + 1, :]
                value = (stream[start : start + 16, :] + conv * jax.nn.sigmoid(conv)) * valid_rows(m, start, 16)
                result[m, start : start + 16, :] = value.astype(BF16)
            relay(m, unit).start()
        return carry

    @pl.when(section > sections // 2)
    def _():
        pass_on()

    lax.fori_loop(0, micro, layer, 0)

    @pl.when(section <= sections // 2)
    def _():
        pass_on()

    @pl.when(first)
    def _():
        for m in range(micro):
            for unit in range(len(units)):
                arrive(m, unit)
            keep(m).start()

    @pl.when(makes_stem)
    def _():
        for m in range(micro):
            stem_copy(m).wait_send()

    for name in ("own", "peer", "out"):
        ring_sent(name)
    for m in range(micro):
        for unit in range(len(units)):
            relay(m, unit).wait_send()
            if unit < DETOURS:
                onward(m, unit).wait_send()
        for side in range(2):
            rim(m, side).wait_send()
            for index in range(len(PIECES)):
                halo(m, index, side).wait_send()
        keep(m).wait()


def shards(sections, nseq, mel, lengths, stem_weight, w_qkv, w_out, norm_gains, conv_kernel):
    micro = mel.shape[0]
    frames = mel.shape[1] // STRIDE
    width = stem_weight.shape[1]
    heads_width = w_qkv.shape[2] // 3
    depth, full_out = w_qkv.shape[1] * 2 * nseq, w_out.shape[1] * 2 * nseq
    steps = nseq // 4
    dma = pltpu.SemaphoreType.DMA
    vmem = pl.BlockSpec(memory_space=pltpu.VMEM)
    arrived = pl.pallas_call(
        functools.partial(kernel, sections, nseq),
        out_shape=jax.ShapeDtypeStruct((micro, frames, width), BF16),
        in_specs=[pl.BlockSpec(memory_space=pltpu.SMEM)] + [vmem] * 6,
        out_specs=pl.BlockSpec(memory_space=pl.ANY),
        scratch_shapes=[
            pltpu.VMEM((stem_weight.shape[0] * 2 * nseq, width), BF16),
            pltpu.VMEM((depth, 3 * heads_width), BF16),
            pltpu.VMEM((full_out, width), BF16),
            pltpu.VMEM(w_out.shape[1:], BF16),
            pltpu.VMEM((2 * micro, frames, width), BF16),
            pltpu.VMEM((frames, width), BF16),
            pltpu.VMEM((micro, 3 * frames, 2 * heads_width), BF16),
            pltpu.VMEM((frames, heads_width), BF16),
            pltpu.VMEM((frames, heads_width), BF16),
            pltpu.VMEM((frames, 3 * frames), F32),
            pltpu.VMEM((HEADS, frames, 3 * frames), F32),
            pltpu.VMEM((frames, width), F32),
            pltpu.VMEM((micro, frames + 16, width), F32),
            pltpu.VMEM((micro, frames, width), BF16),
            pltpu.VMEM((micro, sum(count for _, count in UNITS[:DETOURS]), width), BF16),
            pltpu.VMEM(mel.shape[1:], F32),
            dma((2,)),
            dma((micro,)),
            dma((micro,)),
            dma((3,)),
            dma((3,)),
            dma((4, 2, steps)),
            dma((4, 2, steps)),
            dma((4, 2 * steps)),
            dma((4, 2 * steps)),
            dma((2 * steps,)),
            dma((2 * steps,)),
            dma((micro, len(PIECES), 2)),
            dma((micro, len(PIECES), 2)),
            dma((micro, 2)),
            dma((micro, 2)),
            dma((micro, len(UNITS))),
            dma((micro, len(UNITS))),
            dma((micro, DETOURS)),
            dma((micro, DETOURS)),
            dma((micro,)),
        ],
        compiler_params=pltpu.CompilerParams(
            collective_id=0, has_side_effects=True, vmem_limit_bytes=48 * 1024 * 1024
        ),
    )(lengths, mel, stem_weight, w_qkv[0], w_out[0], norm_gains[0], conv_kernel[0])
    return arrived[None]


def solution(mesh):
    return jax.shard_map(
        functools.partial(shards, mesh.shape["section"], mesh.shape["seq"]),
        mesh=mesh,
        in_specs=(
            P("dp", "seq", None),
            P("dp"),
            P(("seq", "dp"), None),
            P("section", ("seq", "dp"), None),
            P("section", ("seq", "dp"), None),
            P("section", None, None),
            P("section", None, None),
        ),
        out_specs=P("section", "dp", "seq", None),
        check_vma=False,
    )
```

```python
import functools

import jax
import jax.numpy as jnp
from jax import lax
from jax.experimental import pallas as pl
from jax.experimental.pallas import tpu as pltpu
from jax.sharding import PartitionSpec as P

HEADS = 8
STRIDE = 4
UNITS = ((16, 16), (32, 16), (48, 32), (80, 32), (0, 16), (112, 16))
DETOURS = 2
RIM_UNIT = 4
GROUPS = ((2,), (3, 0), (1, 4, 5))
PIECES = tuple(
    (unit, part, parts)
    for group in GROUPS
    for part, parts in (((0, 1), (1, 1)) if group == GROUPS[-1] else ((0, 2),))
    for unit in group
)
eps = 1e-05
masked_score = -1e30
F32 = jnp.float32
BF16 = jnp.bfloat16
MESH = pl.DeviceIdType.MESH


def remote(src, dst, send, recv, **device):
    return pltpu.make_async_remote_copy(
        src_ref=src, dst_ref=dst, send_sem=send, recv_sem=recv, device_id=device, device_id_type=MESH
    )


def rows(ref, start, count):
    return ref.at[pl.ds(pl.multiple_of(start, 16), count)]


def kernel(
    sections, nseq,
    lengths, mel, stem_in, qkv_in, out_in, gains, taps, arrivals,
    stem_full, qkv_full, out_full, out_peer, xs, normed, kv, queries, context, mask, scores, probs_all, stream, conv_in, result, passing,
    mel_wide, local_sem, stem_send, stem_recv, pair_send, pair_recv, ring_send, ring_recv, cross_send, cross_recv, pass_send, pass_recv,
    halo_send, halo_recv, rim_send, rim_recv, relay_send, relay_recv, passing_send, passing_recv, done_sem,
):
    section = lax.axis_index("section")
    seq = lax.axis_index("seq")
    dp = lax.axis_index("dp")
    nz = nseq // 2
    z, core = lax.div(seq, 2), lax.rem(seq, 2)
    ahead = lax.rem(z + 1, nz) * 2 + core
    behind = lax.rem(z + nz - 1, nz) * 2 + core
    other = seq + 1 - 2 * core
    right, left = lax.rem(seq + 1, nseq), lax.rem(seq + nseq - 1, nseq)
    far = jnp.where(core == 1, right, left)
    following, preceding = lax.rem(section + 1, sections), lax.rem(section + sections - 1, sections)
    partner = lax.rem(section + sections // 2, sections)
    beside_following, beside_source = lax.rem(partner + 1, sections), lax.rem(partner + sections - 1, sections)
    first = section == 0
    makes_stem = section == sections // 2 - 1

    micro, frames, width = xs.shape[0] // 2, xs.shape[1], xs.shape[2]
    heads_width = queries.shape[1]
    head_size = heads_width // HEADS
    stem_rows, qkv_rows, out_rows = stem_in.shape[0], qkv_in.shape[0], out_in.shape[0]

    barrier = pltpu.get_barrier_semaphore()
    for device in (
        {"seq": ahead}, {"seq": behind}, {"seq": other}, {"seq": far},
        {"dp": 1 - dp}, {"section": following}, {"section": preceding},
        {"section": partner}, {"section": beside_following}, {"section": beside_source},
    ):
        pl.semaphore_signal(barrier, inc=1, device_id=device, device_id_type=MESH)
    pl.semaphore_wait(barrier, 10)

    def own_rows(full, count):
        return rows(full, (seq * 2 + dp) * count, count)

    stem_pair = remote(stem_in, own_rows(stem_full, stem_rows), pair_send.at[2], pair_recv.at[2], dp=1 - dp)
    stem_keep = pltpu.make_async_copy(stem_in, own_rows(stem_full, stem_rows), local_sem.at[1])
    qkv_pair = remote(qkv_in, own_rows(qkv_full, qkv_rows), pair_send.at[0], pair_recv.at[0], dp=1 - dp)
    qkv_keep = pltpu.make_async_copy(qkv_in, own_rows(qkv_full, qkv_rows), local_sem.at[0])
    out_pair = remote(out_in, out_peer, pair_send.at[1], pair_recv.at[1], dp=1 - dp)

    @pl.when(makes_stem)
    def _():
        stem_pair.start()
        stem_keep.start()

    qkv_pair.start()
    qkv_keep.start()
    out_pair.start()

    steps = nz // 2

    places = [
        [(lax.rem(z + nz - t, nz) * 2 + core) for t in range(steps + 1)],
        [(lax.rem(z + t, nz) * 2 + core) for t in range(steps)],
    ]
    out_cut = out_rows // 16 * 16
    arrays = {
        "stem": (0, stem_full, stem_rows, 0, 2 * stem_rows, stem_rows),
        "own": (1, qkv_full, qkv_rows, dp * qkv_rows, qkv_rows, -(-qkv_rows // 32) * 16),
        "peer": (2, qkv_full, qkv_rows, (1 - dp) * qkv_rows, qkv_rows, qkv_rows),
        "out": (3, out_full, out_rows, 0, 2 * out_rows, out_cut),
    }
    hops, crosses, pairs = {}, {}, {}
    for name, (index, full, count, low, size, cut) in arrays.items():
        for side in range(2):
            for t in ((steps - 2,) if name == "peer" else range(steps)):
                start, length = places[side][t] * (2 * count) + low, size
                if t == steps - 1 and name != "peer":
                    start, length = (start, cut) if side == 0 else (start + cut, size - cut)
                if length:
                    src = rows(full, start, length)
                    hops[name, side, t] = remote(
                        src, src, ring_send.at[index, side, t], ring_recv.at[index, side, t],
                        seq=ahead if side == 0 else behind,
                    )
        for slot in range(2 * steps):
            place = places[0][slot] if slot <= steps else places[1][slot - steps]
            src = rows(full, place * (2 * count) + low, size)
            crosses[name, slot] = remote(src, src, cross_send.at[index, slot], cross_recv.at[index, slot], seq=other)
            if name == "own" and slot not in (0, steps - 1, 2 * steps - 1):
                pairs[slot] = remote(src, src, pass_send.at[slot], pass_recv.at[slot], dp=1 - dp)

    def hop(name, side, t):
        return hops.get((name, side, t))

    def cross(name, slot):
        return crosses[name, slot]

    def ring_open(name):
        for side in range(2):
            if hop(name, side, 0) is not None:
                hop(name, side, 0).start()
        cross(name, 0).start()

    def ring_step(name, t):
        for side in range(2):
            slot = t if side == 0 else steps + t
            hop(name, side, t - 1).wait_recv()
            move = hop(name, side, t)
            if move is not None:
                move.start()
            cross(name, slot).start()
            if name == "own" and slot in pairs:
                pairs[slot].start()

    def ring_close(name):
        for side in range(2):
            move = hop(name, side, steps - 1)
            if move is not None:
                move.wait_recv()
        if name == "own":
            pairs[steps].start()
        if name != "peer":
            cross(name, steps).start()
        if name == "peer":
            for slot in [t + side * steps for t in range(1, steps - 1) for side in range(2)] + [steps]:
                pairs[slot].wait_recv()
                cross(name, slot).start()
                if slot in (steps - 2, 2 * steps - 2):
                    hop(name, slot // steps, steps - 2).start()
            for side in range(2):
                hop(name, side, steps - 2).wait_recv()
                cross(name, steps - 1 + side * steps).start()
        for slot in range(2 * steps):
            cross(name, slot).wait_recv()

    def ring_sent(name):
        for t in range(steps):
            for side in range(2):
                move = hop(name, side, t)
                if move is not None:
                    move.wait_send()
        for slot in range(2 * steps):
            cross(name, slot).wait_send()
            if name == "own" and slot in pairs:
                pairs[slot].wait_send()

    def positions(shape, dim):
        return lax.broadcasted_iota(jnp.int32, shape, dim)

    def valid_rows(m, start, count):
        return jnp.where(positions((count, 1), 0) < lengths[m] - seq * frames - start, 1.0, 0.0)

    def stem_copy(m):
        whole = xs.at[micro + m]
        return remote(whole, whole, stem_send.at[m], stem_recv.at[m], section=beside_following)

    @pl.when(makes_stem)
    def _():
        stem_keep.wait()
        stem_pair.wait()
        ring_open("stem")
        for t in range(1, steps):
            ring_step("stem", t)
        ring_close("stem")
        for m in range(micro):
            mel_wide[...] = mel[m].astype(F32)
            joined = jnp.concatenate(
                [mel_wide[pl.ds(step, frames, stride=STRIDE), :].astype(BF16) for step in range(STRIDE)], axis=1
            )
            for start in range(0, width, 256):
                value = jnp.dot(joined, stem_full[:, start : start + 256], preferred_element_type=F32)
                value = value * jax.nn.sigmoid(value) * valid_rows(m, 0, frames)
                xs[micro + m, :, start : start + 256] = value.astype(BF16)
            stem_copy(m).start()
        ring_sent("stem")

    qkv_keep.wait()
    ring_open("own")

    qkv_pair.wait()
    ring_open("peer")
    out_pair.wait()
    mine, theirs = out_in[...], out_peer[...]
    both = jnp.concatenate(
        [jnp.where(dp == 0, mine, theirs), jnp.where(dp == 0, theirs, mine)], axis=0
    )
    out_full[pl.ds(pl.multiple_of(seq * 2 * out_rows, 16), 2 * out_rows)] = both

    ring_step("own", 1)
    ring_step("own", 2)
    ring_open("out")
    ring_step("own", 3)
    ring_step("out", 1)
    ring_close("own")
    ring_step("out", 2)
    ring_close("peer")
    ring_step("out", 3)

    @pl.when(jnp.logical_not(first))
    def _():
        ring_close("out")


    units = UNITS
    groups = GROUPS

    def relay(m, unit):
        start, count = units[unit]
        src = result.at[m, pl.ds(start, count)]
        if unit < DETOURS:
            dst = passing.at[m, pl.ds(start - units[0][0], count)]
            return remote(src, dst, relay_send.at[m, unit], passing_recv.at[m, unit], section=beside_following)
        dst = xs.at[m, pl.ds(start, count)]
        return remote(src, dst, relay_send.at[m, unit], relay_recv.at[m, unit], section=following)

    def onward(m, unit):
        start, count = units[unit]
        src = passing.at[m, pl.ds(start - units[0][0], count)]
        dst = xs.at[m, pl.ds(start, count)]
        return remote(src, dst, passing_send.at[m, unit], relay_recv.at[m, unit], section=partner)

    def arrive(m, unit):
        (onward if unit < DETOURS else relay)(m, unit).wait_recv()

    def pass_on():
        def one(m, carry):
            for unit in range(DETOURS):
                relay(m, unit).wait_recv()
                onward(m, unit).start()
            return carry

        lax.fori_loop(0, micro, one, 0)

    def halo(m, index, side):
        unit, part, parts = PIECES[index]
        start, count = units[unit]
        columns = pl.ds(part * heads_width, parts * heads_width)
        src = kv.at[m, pl.ds(frames + start, count), columns]
        dst = kv.at[m, pl.ds(2 * frames * side + start, count), columns]
        return remote(
            src, dst, halo_send.at[m, index, side], halo_recv.at[m, index, side], seq=right if side == 0 else left
        )

    near_side, far_side = 1 - core, core
    near_keys = pl.multiple_of(frames * (1 - core), 128)
    far_keys = pl.multiple_of(2 * frames * core, 128)

    def halo_wait(m, side, wanted):
        for index, (unit, part, parts) in enumerate(PIECES):
            if part == wanted:
                start, count = units[unit]
                columns = pl.ds(part * heads_width, parts * heads_width)
                src = kv.at[m, pl.ds(frames + start, count), columns]
                dst = kv.at[m, pl.ds(pl.multiple_of(2 * frames * side + start, 16), count), columns]
                remote(src, dst, halo_send.at[m, index, side], halo_recv.at[m, index, side], seq=right).wait_recv()

    def rim(m, side):
        src = conv_in.at[m, pl.ds(frames if side == 0 else 8, 8)]
        dst = conv_in.at[m, pl.ds(0 if side == 0 else 8 + frames, 8)]
        return remote(src, dst, rim_send.at[m, side], rim_recv.at[m, side], seq=right if side == 0 else left)

    def keep(m):
        return pltpu.make_async_copy(xs.at[m], arrivals.at[m], done_sem.at[m])

    def norm(value, gain):
        average = jnp.mean(value, axis=-1, keepdims=True)
        centered = value - average
        variance = jnp.mean(centered * centered, axis=-1, keepdims=True)
        return centered * lax.rsqrt(variance + eps) * gain

    def layer(m, carry):
        length = lengths[m]
        span = 3 * frames
        query = positions((frames, span), 0)
        column = positions((frames, span), 1)
        key = jnp.where(column < 2 * frames, column + near_keys, column + (far_keys - 2 * frames))
        place = seq * frames - frames + key
        allowed = (place >= 0) & (place < length) & (key >= query) & (key <= query + 2 * frames)
        mask[...] = jnp.where(allowed, 0.0, masked_score).astype(F32)

        slot = jnp.where(first, micro + m, m)

        @pl.when(first)
        def _():
            stem_copy(m).wait_recv()

        for group in groups:
            @pl.when(jnp.logical_not(first))
            def _():
                for unit in group:
                    arrive(m, unit)

            for unit in group:
                for start in range(units[unit][0], sum(units[unit]), 16):
                    value = xs[slot, start : start + 16, :].astype(F32)
                    normed[start : start + 16, :] = norm(value, gains[0:1, :]).astype(BF16)
            some = [normed[units[unit][0] : sum(units[unit]), :] for unit in group]
            some = some[0] if len(some) == 1 else jnp.concatenate(some, axis=0)
            for part in range(2):
                for start in range(part * heads_width, (part + 1) * heads_width, 256):
                    at = heads_width + start
                    value = jnp.dot(some, qkv_full[:, at : at + 256], preferred_element_type=F32).astype(BF16)
                    low = 0
                    for unit in group:
                        at, count = units[unit]
                        kv[m, frames + at : frames + at + count, start : start + 256] = value[low : low + count]
                        low += count
                for index, (unit, first_part, parts) in enumerate(PIECES):
                    if unit in group and first_part + parts - 1 == part:
                        for side in range(2):
                            halo(m, index, side).start()

        @pl.when(jnp.logical_not(first))
        def _():
            keep(m).start()

        for start in range(0, heads_width, 256):
            value = jnp.dot(normed[...], qkv_full[:, start : start + 256], preferred_element_type=F32)
            queries[:, start : start + 256] = value.astype(BF16)
        windows = []
        for h in range(HEADS):
            base, low = h // 4 * 4 * head_size, h % 4 * head_size
            windows.append((base, low, low + head_size, low // 128 * 128, -(-(low + head_size) // 128) * 128))

        def score(first_key, count, at):
            for h, (base, low, high, lane_low, lane_high) in enumerate(windows):
                lane = positions((frames, lane_high - lane_low), 1) + lane_low
                q = queries[:, base + lane_low : base + lane_high]
                q = jnp.where((lane >= low) & (lane < high), q, jnp.zeros_like(q))
                k = kv[m, pl.ds(first_key, count), base + lane_low : base + lane_high]
                scores[h, :, pl.ds(at, count)] = lax.dot_general(
                    q, k, (((1,), (1,)), ((), ())), preferred_element_type=F32
                )

        score(frames, frames, pl.multiple_of(frames * core, 128))
        halo_wait(m, near_side, 0)
        score(pl.multiple_of(2 * frames * (1 - core), 128), frames, pl.multiple_of(frames * (1 - core), 128))
        halo_wait(m, far_side, 0)
        score(far_keys, frames, 2 * frames)

        scale = 1.0 / head_size**0.5
        totals = []
        for h in range(HEADS):
            value = scores[h] * scale + mask[...]
            expon = jnp.exp(value - jnp.max(value, axis=-1, keepdims=True))
            totals.append(jnp.sum(expon, axis=-1, keepdims=True))
            probs_all[h] = expon.astype(BF16)
        halo_wait(m, near_side, 1)
        halo_wait(m, far_side, 1)
        lane = positions((frames, 128), 1)
        for group in range(HEADS // 4):
            outs = []
            for h in range(4 * group, 4 * group + 4):
                base, low, high, lane_low, lane_high = windows[h]
                columns = slice(heads_width + base + lane_low, heads_width + base + lane_high)
                total, probs = totals[h], probs_all[h]
                value = jnp.dot(
                    probs[:, : 2 * frames], kv[m, pl.ds(near_keys, 2 * frames), columns], preferred_element_type=F32
                ) + jnp.dot(
                    probs[:, 2 * frames :], kv[m, pl.ds(far_keys, frames), columns], preferred_element_type=F32
                )
                outs.append(value * (1.0 / total))
            tiles = [
                jnp.where(lane < 96, outs[0], outs[1][:, :128]),
                jnp.where(lane < 64, outs[1][:, 128:], outs[2][:, :128]),
                jnp.where(lane < 32, outs[2][:, 128:], outs[3]),
            ]
            for index, tile in enumerate(tiles):
                at = 4 * head_size * group + index * 128
                context[:, at : at + 128] = tile.astype(BF16)

        @pl.when(first & (m == 0))
        def _():
            ring_close("out")

        for start in range(0, width, 256):
            value = jnp.dot(context[...], out_full[:, start : start + 256], preferred_element_type=F32)
            stream[:, start : start + 256] = value + xs[slot, :, start : start + 256].astype(F32)

        ready = set()

        def prepare(starts):
            for start in starts:
                if start in ready or not 0 <= start < frames:
                    continue
                ready.add(start)
                value = norm(stream[start : start + 16, :], gains[1:2, :]) * valid_rows(m, start, 16)
                conv_in[m, 8 + start : 8 + start + 16, :] = value.astype(BF16).astype(F32)

        prepare((0, frames - 16))
        for side in range(2):
            rim(m, side).start()

        count = taps.shape[0]
        for unit in range(len(units)):
            if unit == RIM_UNIT:
                for side in range(2):
                    rim(m, side).wait_recv()
                top, bottom = conv_in[m, 0:8, :], conv_in[m, 8 + frames : 16 + frames, :]
                conv_in[m, 0:8, :] = jnp.where(seq == 0, 0.0, top)
                conv_in[m, 8 + frames : 16 + frames, :] = jnp.where(seq == nseq - 1, 0.0, bottom)
            for start in range(units[unit][0], sum(units[unit]), 16):
                prepare((start - 16, start, start + 16))
                conv = jnp.zeros((16, width), F32)
                for offset in range(count):
                    at = 8 - count // 2 + start + offset
                    conv = conv + conv_in[m, at : at + 16, :] * taps[offset : offset + 1, :]
                value = (stream[start : start + 16, :] + conv * jax.nn.sigmoid(conv)) * valid_rows(m, start, 16)
                result[m, start : start + 16, :] = value.astype(BF16)
            relay(m, unit).start()
        return carry

    @pl.when(section > sections // 2)
    def _():
        pass_on()

    lax.fori_loop(0, micro, layer, 0)

    @pl.when(section <= sections // 2)
    def _():
        pass_on()

    @pl.when(first)
    def _():
        for m in range(micro):
            for unit in range(len(units)):
                arrive(m, unit)
            keep(m).start()

    @pl.when(makes_stem)
    def _():
        for m in range(micro):
            stem_copy(m).wait_send()

    for name in ("own", "peer", "out"):
        ring_sent(name)
    for m in range(micro):
        for unit in range(len(units)):
            relay(m, unit).wait_send()
            if unit < DETOURS:
                onward(m, unit).wait_send()
        for side in range(2):
            rim(m, side).wait_send()
            for index in range(len(PIECES)):
                halo(m, index, side).wait_send()
        keep(m).wait()


def shards(sections, nseq, mel, lengths, stem_weight, w_qkv, w_out, norm_gains, conv_kernel):
    micro = mel.shape[0]
    frames = mel.shape[1] // STRIDE
    width = stem_weight.shape[1]
    heads_width = w_qkv.shape[2] // 3
    depth, full_out = w_qkv.shape[1] * 2 * nseq, w_out.shape[1] * 2 * nseq
    steps = nseq // 4
    dma = pltpu.SemaphoreType.DMA
    vmem = pl.BlockSpec(memory_space=pltpu.VMEM)
    arrived = pl.pallas_call(
        functools.partial(kernel, sections, nseq),
        out_shape=jax.ShapeDtypeStruct((micro, frames, width), BF16),
        in_specs=[pl.BlockSpec(memory_space=pltpu.SMEM)] + [vmem] * 6,
        out_specs=pl.BlockSpec(memory_space=pl.ANY),
        scratch_shapes=[
            pltpu.VMEM((stem_weight.shape[0] * 2 * nseq, width), BF16),
            pltpu.VMEM((depth, 3 * heads_width), BF16),
            pltpu.VMEM((full_out, width), BF16),
            pltpu.VMEM(w_out.shape[1:], BF16),
            pltpu.VMEM((2 * micro, frames, width), BF16),
            pltpu.VMEM((frames, width), BF16),
            pltpu.VMEM((micro, 3 * frames, 2 * heads_width), BF16),
            pltpu.VMEM((frames, heads_width), BF16),
            pltpu.VMEM((frames, heads_width), BF16),
            pltpu.VMEM((frames, 3 * frames), F32),
            pltpu.VMEM((HEADS, frames, 3 * frames), F32),
            pltpu.VMEM((HEADS, frames, 3 * frames), BF16),
            pltpu.VMEM((frames, width), F32),
            pltpu.VMEM((micro, frames + 16, width), F32),
            pltpu.VMEM((micro, frames, width), BF16),
            pltpu.VMEM((micro, sum(count for _, count in UNITS[:DETOURS]), width), BF16),
            pltpu.VMEM(mel.shape[1:], F32),
            dma((2,)),
            dma((micro,)),
            dma((micro,)),
            dma((3,)),
            dma((3,)),
            dma((4, 2, steps)),
            dma((4, 2, steps)),
            dma((4, 2 * steps)),
            dma((4, 2 * steps)),
            dma((2 * steps,)),
            dma((2 * steps,)),
            dma((micro, len(PIECES), 2)),
            dma((micro, len(PIECES), 2)),
            dma((micro, 2)),
            dma((micro, 2)),
            dma((micro, len(UNITS))),
            dma((micro, len(UNITS))),
            dma((micro, DETOURS)),
            dma((micro, DETOURS)),
            dma((micro,)),
        ],
        compiler_params=pltpu.CompilerParams(
            collective_id=0, has_side_effects=True, vmem_limit_bytes=48 * 1024 * 1024
        ),
    )(lengths, mel, stem_weight, w_qkv[0], w_out[0], norm_gains[0], conv_kernel[0])
    return arrived[None]


def solution(mesh):
    return jax.shard_map(
        functools.partial(shards, mesh.shape["section"], mesh.shape["seq"]),
        mesh=mesh,
        in_specs=(
            P("dp", "seq", None),
            P("dp"),
            P(("seq", "dp"), None),
            P("section", ("seq", "dp"), None),
            P("section", ("seq", "dp"), None),
            P("section", None, None),
            P("section", None, None),
        ),
        out_specs=P("section", "dp", "seq", None),
        check_vma=False,
    )
```
